128 devices in a mesh: ctx: 32 (over x, y, z_lo), fsdp: 4 (over z_hi, core).
Axes of the slice: x: 4, y: 4, z: 4 (z_hi: 2, z_lo: 2; z = z_hi * 2 + z_lo), core: 2. Of those that a mesh axis runs over, the one named last changes fastest.
Arguments:
- hidden: bfloat16 [16384, 768], P(('ctx', 'fsdp')), may hold values from -6 to 6
- qkv_weight: bfloat16 [768, 2304], P('fsdp'), may hold values from -0.21875 to 0.21875
- qkv_bias: bfloat16 [2304], P('fsdp'), may hold values from -3 to 3
- dense_weight: bfloat16 [768, 768], P('fsdp'), may hold values from -1.75 to 1.75
- dense_bias: bfloat16 [768], P('fsdp'), may hold values from -3 to 3
- up_weight: bfloat16 [768, 3072], P('fsdp'), may hold values from -0.21875 to 0.21875
- up_bias: bfloat16 [3072], P('fsdp'), may hold values from -3 to 3
- down_weight: bfloat16 [3072, 768], P('fsdp'), may hold values from -0.109375 to 0.109375
- down_bias: bfloat16 [768], P('fsdp'), may hold values from -3 to 3
- attn_gain: bfloat16 [768], P('fsdp'), may hold values from 0.5 to 1.5
- attn_shift: bfloat16 [768], P('fsdp'), may hold values from -2 to 2
- mlp_gain: bfloat16 [768], P('fsdp'), may hold values from 0.5 to 1.5
- mlp_shift: bfloat16 [768], P('fsdp'), may hold values from -2 to 2
- block_table: int32 [32, 2], replicated, may hold values from 0 to 63, as said below
- cotangent: bfloat16 [16384, 768], P(('ctx', 'fsdp')), may hold values from -6 to 6
Outputs:
- layer_out: bfloat16 [16384, 768], P(('ctx', 'fsdp'))
- input_grad: bfloat16 [16384, 768], P(('ctx', 'fsdp'))
- qkv_weight_grad: float32 [768, 2304], P(('ctx', 'fsdp'))
- qkv_bias_grad: float32 [768, 3], P(('ctx', 'fsdp'))
- dense_weight_grad: float32 [768, 768], P(('ctx', 'fsdp'))
- dense_bias_grad: float32 [768], P(('ctx', 'fsdp'))
- up_weight_grad: float32 [768, 3072], P(('ctx', 'fsdp'))
- up_bias_grad: float32 [3072], P(('ctx', 'fsdp'))
- down_weight_grad: float32 [3072, 768], P(('ctx', 'fsdp'))
- down_bias_grad: float32 [768], P(('ctx', 'fsdp'))
- attn_gain_grad: float32 [768], P(('ctx', 'fsdp'))
- attn_shift_grad: float32 [768], P(('ctx', 'fsdp'))
- mlp_gain_grad: float32 [768], P(('ctx', 'fsdp'))
- mlp_shift_grad: float32 [768], P(('ctx', 'fsdp'))
The draws below stay inside these ranges and needn't reach their ends.
Inputs may be any that keep to these rules, and one draw needn't show every extreme that they name: `block_table`: row c holds the early block of ctx index c and then its late partner: every block 0 .. 63 appears once, and the second entry is 63 minus the first.
All inputs are finite; a program needn't handle non-finite values.
Results may differ from the reference program's by a relative error of at most 0.035.
Values may be sent and summed in bfloat16 or wider, within the bound.
No kernel may reach another device: no remote copies, remote signals or barrier semaphores. Data moves between devices by JAX's collectives and lax.ppermute only.
A program may use at most 192 MiB of HBM per device.

```python
from functools import partial
import jax
import jax.numpy as jnp
from jax import lax

D = 768
HEADS = 12
HEAD = 64
ROT = 16
FF = 3072
TOK_DEV = 128
TOKENS = 16384
N_CTX = 32
N_FSDP = 4


def draw_block_table(key, part):
    key = jax.random.fold_in(key, 7)
    early_ids = jax.random.permutation(key, N_CTX).astype(jnp.int32)
    return jnp.stack([early_ids, 2 * N_CTX - 1 - early_ids], axis=1).astype(jnp.int32)


def steps_of(key, shape, shards, smallest, top_value):
    loudness = 1.0
    for dim, shards_of in shards:
        heights = jax.random.uniform(jax.random.fold_in(jax.random.fold_in(key, 6), dim), (shards_of,), jnp.float32, smallest / len(shards), top_value / len(shards))
        loudness = loudness * jnp.repeat(jnp.exp(heights), shape[dim] // shards_of).reshape((-1,) + (1,) * (len(shape) - 1 - dim))
    return loudness


def noise(stream_key, shape, scale, reach, split=(), kind=jnp.bfloat16):
    array = scale * jax.random.normal(stream_key, shape, jnp.float32)
    if split:
        array = array * steps_of(stream_key, shape, split, -0.22, 0.18)
    return jnp.clip(array, -reach, reach).astype(kind)


def setup_inputs(seed: int = 0) -> dict:
    key_of = jax.random.split(jax.random.key(seed), 16)
    return {
        "hidden": noise(key_of[0], (TOKENS, D), 1.0, 6.0, ((0, 128),)),
        "qkv_weight": noise(key_of[1], (D, 3 * D), D ** -0.5, 0.21875, ((0, 4),)),
        "qkv_bias": noise(key_of[2], (3 * D,), 0.5, 3.0, ((0, 4),)),
        "dense_weight": noise(key_of[3], (D, D), (D // 64) ** -0.5, 1.75, ((0, 4),)),
        "dense_bias": noise(key_of[4], (D,), 0.5, 3.0, ((0, 4),)),
        "up_weight": noise(key_of[5], (D, FF), D ** -0.5, 0.21875, ((0, 4),)),
        "up_bias": noise(key_of[6], (FF,), 0.5, 3.0, ((0, 4),)),
        "down_weight": noise(key_of[7], (FF, D), FF ** -0.5, 0.109375, ((0, 4),)),
        "down_bias": noise(key_of[8], (D,), 0.5, 3.0, ((0, 4),)),
        "attn_gain": jnp.clip(1.0 + 0.1 * jax.random.normal(key_of[9], (D,), jnp.float32), 0.5, 1.5).astype(jnp.bfloat16),
        "attn_shift": noise(key_of[10], (D,), 0.3, 2.0, ((0, 4),)),
        "mlp_gain": jnp.clip(1.0 + 0.1 * jax.random.normal(key_of[11], (D,), jnp.float32), 0.5, 1.5).astype(jnp.bfloat16),
        "mlp_shift": noise(key_of[12], (D,), 0.3, 2.0, ((0, 4),)),
        "block_table": draw_block_table(jax.random.fold_in(key_of[15], 71), 0),
        "cotangent": noise(key_of[14], (TOKENS, D), 1.0, 6.0, ((0, 128),)),
    }


@jax.custom_vjp
def low(v):
    return lax.optimization_barrier(v.astype(jnp.bfloat16)).astype(jnp.float32)

@jax.custom_vjp
def low_back(v):
    return v

def low_keep(v):
    return (low(v), None)

def low_pass(kept, grad):
    return (grad,)

def back_keep(v):
    return (v, None)

def back_low(kept, grad):
    return (low(grad),)
low.defvjp(low_keep, low_pass)
low_back.defvjp(back_keep, back_low)
norm_eps = 1e-05
masked_value = -1e+30

def matmul_high(left_side, right_side):
    return jnp.dot(left_side, right_side, precision=lax.Precision.HIGHEST, preferred_element_type=jnp.float32)

def layer_norm(values, norm_gain, norm_shift):
    center = lax.optimization_barrier(jnp.mean(values, axis=-1, keepdims=True))
    centered = values - center
    spread = lax.optimization_barrier(jnp.mean(centered * centered, axis=-1, keepdims=True))
    return centered * lax.rsqrt(spread + norm_eps) * norm_gain + norm_shift

def rotate(tensor, cosine, sine_table):
    half_dims = ROT // 2
    upper_half = tensor[..., :half_dims]
    lower_half = tensor[..., half_dims:ROT]
    return jnp.concatenate([upper_half * cosine - lower_half * sine_table, lower_half * cosine + upper_half * sine_table, tensor[..., ROT:]], axis=-1)

def token_positions(block_table):
    row_ids = jnp.arange(TOKENS, dtype=jnp.int32)
    half_rows = TOK_DEV // 2
    device_ids = row_ids // TOK_DEV
    within = row_ids % TOK_DEV
    ctx_ids = device_ids // N_FSDP
    fsdp_ids = device_ids % N_FSDP
    block_ids = block_table[ctx_ids, within // half_rows].astype(jnp.int32)
    return (block_ids * (half_rows * N_FSDP) + fsdp_ids * half_rows + within % half_rows).astype(jnp.int32)

def attend_block(inputs, key_all, value_all, key_pos):
    queries, query_pos = inputs
    score_scale = HEAD ** (-0.5)
    scores = low_back(jnp.einsum('qhd,khd->qhk', queries, key_all, precision=lax.Precision.HIGHEST) * score_scale)
    visible = key_pos[None, None, :] <= query_pos[:, None, None]
    masked = jnp.where(visible, scores, masked_value)
    highest = lax.optimization_barrier(jnp.max(masked, axis=-1, keepdims=True))
    weights = jnp.where(visible, jnp.exp(masked - highest), 0.0)
    attn_probs = low(weights / lax.optimization_barrier(jnp.sum(weights, axis=-1, keepdims=True)))
    return jnp.einsum('qhk,khd->qhd', attn_probs, value_all, precision=lax.Precision.HIGHEST)

def layer_forward(hidden, qkv_weight, qkv_bias, dense_weight, dense_bias, up_weight, up_bias, down_weight, down_bias, attn_gain, attn_shift, mlp_gain, mlp_shift, cosine, sine_table, positions):
    first_in = low(layer_norm(hidden, attn_gain, attn_shift))
    second_in = low(layer_norm(hidden, mlp_gain, mlp_shift))
    projected = low_back(matmul_high(first_in, qkv_weight) + qkv_bias).reshape(TOKENS, 3, HEADS, HEAD)
    queries = low(low_back(rotate(projected[:, 0], cosine, sine_table)))
    key_all = low(low_back(rotate(projected[:, 1], cosine, sine_table)))
    value_all = low(low_back(projected[:, 2]))
    span_rows = min(TOKENS, 512)
    block_count = TOKENS // span_rows
    attend = jax.checkpoint(partial(attend_block, key_all=key_all, value_all=value_all, key_pos=positions))
    attended = lax.map(attend, (queries.reshape(block_count, span_rows, HEADS, HEAD), positions.reshape(block_count, span_rows)))
    attended = low(low_back(attended.reshape(TOKENS, D)))
    attn_out = matmul_high(attended, dense_weight) + dense_bias
    pre_act = low_back(matmul_high(second_in, up_weight) + up_bias)
    activated = low(jax.nn.gelu(pre_act, approximate=False))
    mlp_out = matmul_high(activated, down_weight) + down_bias
    return hidden + attn_out + mlp_out

def reference(hidden, qkv_weight, qkv_bias, dense_weight, dense_bias, up_weight, up_bias, down_weight, down_bias, attn_gain, attn_shift, mlp_gain, mlp_shift, block_table, cotangent):
    positions = token_positions(block_table)
    frequency = jnp.power(10000.0, -jnp.arange(0, ROT, 2, dtype=jnp.float32) / ROT)
    angles = positions.astype(jnp.float32)[:, None] * frequency[None, :]
    cosine = jnp.cos(angles)[:, None, :]
    sine_table = jnp.sin(angles)[:, None, :]

    def closed(*operands):
        return layer_forward(*operands, cosine, sine_table, positions)
    operands = (hidden, qkv_weight, qkv_bias, dense_weight, dense_bias, up_weight, up_bias, down_weight, down_bias, attn_gain, attn_shift, mlp_gain, mlp_shift)
    operands = tuple((tensor.astype(jnp.float32) for tensor in operands))
    layer_out, pullback = jax.vjp(closed, *operands)
    gradients = pullback(cotangent.astype(jnp.float32))
    bias_parts = gradients[2].reshape(3, D).T
    return (layer_out.astype(jnp.bfloat16), gradients[0].astype(jnp.bfloat16), gradients[1], bias_parts, gradients[3], gradients[4], gradients[5], gradients[6], gradients[7], gradients[8], gradients[9], gradients[10], gradients[11], gradients[12])
```

```python
import math

import jax
import jax.numpy as jnp
import numpy as np
from jax import lax
from jax.experimental import pallas as pl
from jax.experimental.pallas import tpu as pltpu
from jax.sharding import Mesh, PartitionSpec as P

D = 768
HEADS = 12
HEAD = 64
ROT = 16
GROUP = 4
OWN = HEADS // GROUP
WIDE = D // GROUP
LANES = 128
SUB = 128
BLOCK = 256
SPAN = 4
AXES = ("x", "y", "zl", "zh", "c")
SIZES = (4, 4, 2, 2, 2)
PLANE = ("x", "y", "c")
norm_eps = 1e-05
masked_value = -1e30


def lane_tables():
    spread = np.zeros((3 * WIDE, 2 * D), np.float32)
    partner = np.zeros((D, D), np.float32)
    for head in range(OWN):
        for lane in range(HEAD):
            source = head * HEAD + lane
            swapped = head * HEAD + (lane ^ (ROT // 2))
            q_lane = head * LANES + lane
            k_lane = OWN * LANES + q_lane
            spread[source, q_lane] = 1
            spread[WIDE + source, k_lane] = 1
            spread[2 * WIDE + source, k_lane + HEAD] = 1
            if lane < ROT:
                spread[swapped, D + q_lane] = 1
                spread[WIDE + swapped, D + k_lane] = 1
                partner[q_lane ^ (ROT // 2), q_lane] = 1
                partner[k_lane ^ (ROT // 2), k_lane] = 1
    late_half = np.zeros((WIDE, OWN * LANES), np.float32)
    for head in range(OWN):
        for lane in range(HEAD):
            late_half[head * HEAD + lane, head * LANES + HEAD + lane] = 1
    return tuple(t.astype(jnp.bfloat16) for t in (spread, partner, late_half))


SPREAD, PARTNER, LATE_HALF = lane_tables()


def dot(a, b):
    return jnp.dot(a, b, preferred_element_type=jnp.float32)


def outer_sum(a, b):
    return lax.dot_general(a, b, (((0,), (0,)), ((), ())), preferred_element_type=jnp.float32)


def times_transposed(a, b):
    return lax.dot_general(a, b, (((1,), (1,)), ((), ())), preferred_element_type=jnp.float32)


def attend_head(
    order, flips, ends, source, q_pos, q_in, g_in, kv, out, dq, dkv,
    kv_turned, q_rows, q_cols, g_rows, g_cols, col_pos, dq_sum,
):
    subs = kv.shape[0]
    blocks = subs // 2
    lanes = q_in.shape[0]
    keys = SPAN * BLOCK
    last_span = [ends[s] // SPAN for s in range(4)]

    def places(span):
        for i in range(SPAN):
            at = order[span * SPAN + i]
            yield at
            yield at + 4

    def load(span):
        return jnp.concatenate([kv[at] for at in places(span)], axis=0)

    def load_turned(span, first):
        return jnp.concatenate([kv_turned[at, first : first + HEAD] for at in places(span)], axis=1)

    def turn(i, carry):
        kv_turned[i] = kv[i].T
        return carry

    lax.fori_loop(0, subs, turn, 0)
    for s in range(4):
        rows = pl.ds(pl.multiple_of(source[s] * SUB, SUB), SUB)
        here = slice(s * SUB, (s + 1) * SUB)
        q_rows[here] = q_in[rows]
        g_rows[here] = g_in[rows]
        q_cols[:, here] = q_in[rows].T
        g_cols[:, here] = g_in[rows].T
        col_pos[:, here] = q_pos[:, rows]

    def visible(span, first):
        row = lax.broadcasted_iota(jnp.int32, (BLOCK, 1), 0)
        core, member, within = row // SUB, row % SUB // HEAD, row % HEAD
        parts = []
        for i in range(SPAN):
            block = span * SPAN + i
            flip = flips[block]
            piece = 2 * (member + flip - 2 * flip * member) + core
            parts.append(block * BLOCK + piece * HEAD + within)
        return jnp.concatenate(parts, axis=0) <= col_pos[:, first:]

    def regions(make, carry):
        done = 0
        for s in range(4):
            first = s * SUB
            state = tuple(c[:, first:] for c in carry)
            state = lax.fori_loop(done, last_span[s], make(first, False), state)
            state = lax.fori_loop(jnp.maximum(done, last_span[s]), last_span[s] + 1, make(first, True), state)
            done = last_span[s] + 1
            carry = tuple(jnp.concatenate([c[:, :first], n], axis=1) if first else n for c, n in zip(carry, state))
        return carry

    def forward(first, masked):
        def step(span, carry):
            top, total, acc = carry
            scores = dot(load(span), q_cols[:, first:])
            if masked:
                scores = jnp.where(visible(span, first), scores, masked_value)
            new_top = jnp.maximum(top, jnp.max(scores, axis=0, keepdims=True))
            weights = jnp.exp(scores - new_top)
            factor = jnp.exp(top - new_top)
            total = total * factor + jnp.sum(weights, axis=0, keepdims=True)
            acc = acc * factor + dot(load_turned(span, HEAD), weights.astype(jnp.bfloat16))
            return new_top, total, acc

        return step

    top, total, acc = regions(
        forward,
        (
            jnp.full((1, lanes), masked_value, jnp.float32),
            jnp.zeros((1, lanes), jnp.float32),
            jnp.zeros((HEAD, lanes), jnp.float32),
        ),
    )
    attended = acc / total
    log_total = top + jnp.log(total)
    delta = jnp.sum(attended * g_cols[HEAD:].astype(jnp.float32), axis=0, keepdims=True)
    dq_sum[...] = jnp.zeros_like(dq_sum)

    def backward(first, masked):
        def step(span, carry):
            key_value = load(span)
            scores = dot(key_value, q_cols[:, first:])
            probs = jnp.exp(scores - log_total[:, first:])
            if masked:
                probs = jnp.where(visible(span, first), probs, 0.0)
            grad_probs = dot(key_value, g_cols[:, first:])
            grad_scores = (probs * (grad_probs - delta[:, first:])).astype(jnp.bfloat16)
            both = dot(grad_scores, q_rows[first:]) + dot(probs.astype(jnp.bfloat16), g_rows[first:])
            both = both.astype(dkv.dtype)
            for i, at in enumerate(places(span)):
                dkv[at] = both[i * SUB : (i + 1) * SUB]
            dq_sum[:HEAD, first:] += dot(load_turned(span, 0), grad_scores)
            return carry

        return step

    regions(backward, ())

    def clear(span, carry):
        for at in places(span):
            dkv[at] = jnp.zeros((SUB, 2 * HEAD), dkv.dtype)
        return carry

    lax.fori_loop(last_span[3] + 1, blocks // SPAN, clear, 0)
    for s in range(4):
        rows = pl.ds(pl.multiple_of(source[s] * SUB, SUB), SUB)
        here = slice(s * SUB, (s + 1) * SUB)
        out[:, rows] = attended[:, here]
        dq[rows] = (dq_sum[:, here].T * HEAD**-0.5).astype(dq.dtype)


def attend(order, flips, ends, source, q_pos, queries, grads, kv):
    rows, width = queries.shape
    heads = width // 128
    smem = pl.BlockSpec(memory_space=pltpu.SMEM)
    tokens = pl.BlockSpec((rows, 128), lambda h: (0, h))
    whole = pl.BlockSpec((kv.shape[0], SUB, 128), lambda h: (0, 0, h))
    return pl.pallas_call(
        attend_head,
        grid=(heads,),
        out_shape=(
            jax.ShapeDtypeStruct((heads * HEAD, rows), jnp.float32),
            jax.ShapeDtypeStruct(queries.shape, jnp.bfloat16),
            jax.ShapeDtypeStruct(kv.shape, jnp.bfloat16),
        ),
        in_specs=[smem] * 4 + [pl.BlockSpec((1, rows), lambda h: (0, 0)), tokens, tokens, whole],
        out_specs=(pl.BlockSpec((HEAD, rows), lambda h: (h, 0)), tokens, whole),
        scratch_shapes=[
            pltpu.VMEM((kv.shape[0], 128, SUB), jnp.bfloat16),
            pltpu.VMEM((rows, 128), jnp.bfloat16),
            pltpu.VMEM((128, rows), jnp.bfloat16),
            pltpu.VMEM((rows, 128), jnp.bfloat16),
            pltpu.VMEM((128, rows), jnp.bfloat16),
            pltpu.VMEM((1, rows), jnp.int32),
            pltpu.VMEM((128, rows), jnp.float32),
        ],
        compiler_params=pltpu.CompilerParams(vmem_limit_bytes=50 * 1024 * 1024),
    )(order, flips, ends, source, q_pos, queries, grads, kv)


def norm_parts(values):
    center = jnp.mean(values, axis=-1, keepdims=True)
    centered = values - center
    spread = jnp.mean(centered * centered, axis=-1, keepdims=True)
    inverse = lax.rsqrt(spread + norm_eps)
    return centered * inverse, inverse


def norm_backward(grad_out, normed, inverse, norm_gain):
    scaled = grad_out * norm_gain
    return inverse * (
        scaled
        - jnp.mean(scaled, axis=-1, keepdims=True)
        - normed * jnp.mean(scaled * normed, axis=-1, keepdims=True)
    )


def shifted(a, step):
    def target(zl, zh):
        there = (2 * zh + zl + step) % 4
        return (there % 2, there // 2)

    return moved(a, ("zl", "zh"), target)


def other_core(a):
    return lax.ppermute(a, "c", [(0, 1), (1, 0)])


def other_high(a):
    return lax.ppermute(a, "zh", [(0, 1), (1, 0)])


def moved(a, names, target):
    sizes = [SIZES[AXES.index(n)] for n in names]
    pairs = []
    for index in range(int(np.prod(sizes))):
        there = target(*np.unravel_index(index, sizes))
        pairs.append((index, int(np.ravel_multi_index(there, sizes))))
    return lax.ppermute(a, names, pairs)


def in_order(parts, high, low):
    a, b, c, d = parts
    a, b = jnp.where(low == 0, a, b), jnp.where(low == 0, b, a)
    c, d = jnp.where(low == 0, c, d), jnp.where(low == 0, d, c)
    return (
        jnp.where(high == 0, a, c),
        jnp.where(high == 0, b, d),
        jnp.where(high == 0, c, a),
        jnp.where(high == 0, d, b),
    )


def token_rows(parts):
    rows, width = parts[0].shape
    stacked = jnp.stack(parts).reshape(2, 2, 2, rows // 2, width)
    return stacked.transpose(0, 2, 1, 3, 4).reshape(4 * rows, width)


def gathered_tokens(own):
    return token_rows([own, shifted(own, 2), shifted(own, 1), shifted(own, -1)])


def scattered_tokens(total):
    rows, width = total.shape
    parts = total.reshape(2, 2, 2, rows // 8, width).transpose(0, 2, 1, 3, 4).reshape(4, rows // 4, width)
    sent = parts[1:].astype(jnp.bfloat16)
    return (
        parts[0]
        + shifted(sent[0], 2).astype(jnp.float32)
        + shifted(sent[1], -1).astype(jnp.float32)
        + shifted(sent[2], 1).astype(jnp.float32)
    )


def gathered_keys(own):
    whole = lax.all_gather(own, PLANE, axis=0, tiled=True)
    return whole.reshape(-1, SUB, own.shape[1])


def scattered_keys(grads):
    return lax.psum_scatter(grads.reshape(-1, grads.shape[-1]), PLANE, scatter_dimension=0, tiled=True)


def plane_sum(chunks, core):
    count, rows, width = chunks.shape
    pairs = chunks.astype(jnp.bfloat16).reshape(count // 2, 2, rows, width)
    sent = jnp.where(core == 0, pairs[:, 1], pairs[:, 0])
    kept = jnp.where(core == 0, pairs[:, 0], pairs[:, 1])
    chip = (kept.astype(jnp.float32) + other_core(sent).astype(jnp.float32)).astype(jnp.bfloat16)
    parts = lax.all_to_all(chip, ("x", "y"), split_axis=0, concat_axis=0, tiled=True)
    return jnp.sum(parts.astype(jnp.float32), axis=0)


def to_row_owners(rows, slice_index, high, core):
    pieces = rows.reshape(GROUP, -1, rows.shape[1])
    got = []
    for j in range(GROUP):
        piece = lax.dynamic_index_in_dim(pieces, jnp.bitwise_xor(j, slice_index), 0, keepdims=False)

        def target(zl, zh, c, j=j):
            k = j ^ (2 * zh + zl)
            return (c, k // 2, k % 2)

        got.append(moved(piece, ("zl", "zh", "c"), target))
    return in_order(got, high, core)


def to_block_owners(block):
    return moved(block, AXES, lambda x, y, zl, zh, c: (2 * zh + zl, x, y // 2, y % 2, c))


def local(
    hidden,
    qkv_weight,
    qkv_bias,
    dense_weight,
    dense_bias,
    up_weight,
    up_bias,
    down_weight,
    down_bias,
    attn_gain,
    attn_shift,
    mlp_gain,
    mlp_shift,
    block_table,
    cotangent,
):
    x, y, low, high, core = (lax.axis_index(a) for a in AXES)
    depth = 2 * high + low
    tok_rows = hidden.shape[0]
    half_rows = tok_rows // 2
    own_slice = core == low

    tokens = gathered_tokens(hidden)
    cot = gathered_tokens(cotangent)

    def columns(index):
        qkv = lax.dynamic_index_in_dim(qkv_weight.reshape(-1, 3, GROUP, WIDE), index, 2, keepdims=False)
        up = lax.dynamic_slice_in_dim(up_weight, index * D, D, 1)
        return jnp.concatenate([qkv.reshape(-1, 3 * WIDE), up], axis=1)

    mine, theirs = columns(depth), other_high(columns(2 * (1 - high) + low))
    both = jnp.stack([jnp.where(high == 0, mine, theirs), jnp.where(high == 0, theirs, mine)])
    swapped = other_core(both)
    by_rows = jnp.stack([jnp.where(core == 0, both, swapped), jnp.where(core == 0, swapped, both)], axis=1)
    by_rows = by_rows.reshape(D, 3 * WIDE + D)
    qkv_slice, up_slice = by_rows[:, : 3 * WIDE], by_rows[:, 3 * WIDE :]
    shards = jnp.concatenate([down_weight, dense_weight], axis=0)
    shards = jnp.where(own_slice, shards, other_core(shards))
    down_slice, dense_slice = shards[:D], shards[D:]

    small = jnp.concatenate(
        [qkv_bias, up_bias, dense_bias, down_bias, attn_gain, attn_shift, mlp_gain, mlp_shift]
    ).reshape(1, -1)
    from_core = other_core(small)
    from_high = other_high(small)
    from_both = moved(small, ("zh", "c"), lambda zh, c: (1 - zh, 1 - c))
    small_all = jnp.concatenate(in_order([small, from_core, from_high, from_both], high, core), axis=0)
    small_all = small_all.astype(jnp.float32)
    up_at = 3 * WIDE
    up_bias_slice = jnp.where(own_slice, small, from_core)[0, up_at : up_at + D].astype(jnp.float32)
    qkv_bias_all = small_all[:, : 3 * WIDE].reshape(3, GROUP, WIDE)
    qkv_bias_slice = lax.dynamic_index_in_dim(qkv_bias_all, depth, 1, keepdims=False).reshape(1, -1)
    vectors = [small_all[:, at : at + WIDE].reshape(D) for at in range(up_at + D, small.shape[1], WIDE)]
    dense_bias_all, down_bias_all, attn_gain_all, attn_shift_all, mlp_gain_all, mlp_shift_all = vectors

    members = [depth, (depth + 2) % 4, (depth + 3) % 4, (depth + 1) % 4]
    piece = 2 * (jnp.stack(members).reshape(2, 2) // 2) + core
    ctx = x * 8 + y * 2 + jnp.stack([low, 1 - low])
    own_blocks = block_table[ctx]
    positions = (
        own_blocks[:, :, None, None] * BLOCK
        + piece[:, None, :, None] * half_rows
        + jnp.arange(half_rows, dtype=jnp.int32)
    ).reshape(-1)
    flat = block_table.reshape(-1)
    count = flat.shape[0]
    ids = jnp.arange(count, dtype=jnp.int32)
    place = jnp.sum(jnp.where(flat[None, :] == ids[:, None], ids[None, :], 0), axis=1)
    pair = jnp.bitwise_xor((place // 2) % 2, low)
    order = (place // 4) * 8 + pair * 2 + place % 2
    flips = jnp.where(pair == 0, members[0] // 2, members[2] // 2)
    first = jnp.where(own_blocks[0, 0] < own_blocks[1, 0], 0, 1)
    ends = jnp.sort(own_blocks.reshape(-1))
    source = jnp.stack([2 * first, 2 - 2 * first, 3 - 2 * first, 2 * first + 1]).astype(jnp.int32)
    rotary = 10000.0 ** (-np.arange(0, ROT, 2, dtype=np.float64) / ROT)
    frequency = np.zeros((1, LANES), np.float32)
    frequency[0, :ROT] = np.concatenate([rotary, rotary])
    sign = np.zeros((1, LANES), np.float32)
    sign[0, :ROT] = np.repeat([-1.0, 1.0], ROT // 2)
    angles = positions.astype(jnp.float32)[:, None] * frequency
    cosine = jnp.concatenate([jnp.cos(angles)] * 6, axis=1)
    sine = jnp.concatenate([jnp.sin(angles) * sign] * 6, axis=1)

    normed, _ = norm_parts(tokens.astype(jnp.float32))
    first_in = (normed * attn_gain_all + attn_shift_all).astype(jnp.bfloat16)
    second_in = (normed * mlp_gain_all + mlp_shift_all).astype(jnp.bfloat16)
    spread_weight = dot(qkv_slice, SPREAD).astype(jnp.bfloat16)
    spread_bias = dot(qkv_bias_slice.astype(jnp.bfloat16), SPREAD)
    projected = dot(first_in, spread_weight) + spread_bias
    turned = projected[:, :D] * cosine + projected[:, D:] * sine
    queries = (turned[:, : OWN * LANES] * HEAD**-0.5).astype(jnp.bfloat16)
    key_value = turned[:, OWN * LANES :].astype(jnp.bfloat16)
    key_all = gathered_keys(key_value)

    pre_act = dot(second_in, up_slice) + up_bias_slice
    cdf_part = 0.5 * (1.0 + lax.erf(pre_act * (1.0 / math.sqrt(2.0))))
    density = jnp.exp(-0.5 * pre_act * pre_act) * (1.0 / math.sqrt(2.0 * math.pi))
    activated = (pre_act * cdf_part).astype(jnp.bfloat16)
    grad_act = times_transposed(cot, down_slice)
    grad_pre_wide = grad_act * (cdf_part + pre_act * density)
    grad_pre = grad_pre_wide.astype(jnp.bfloat16)
    grad_up = outer_sum(second_in, grad_pre)
    grad_down = outer_sum(activated, cot)
    grad_up_bias = jnp.sum(grad_pre.astype(jnp.float32), axis=0)
    bias_grad = jnp.sum(cot.astype(jnp.float32), axis=0)
    second_part = times_transposed(grad_pre, up_slice)
    mlp_part = dot(activated, down_slice)
    early = jnp.concatenate([grad_up.reshape(32, -1, D), grad_down.reshape(32, -1, D)], axis=1)
    early = plane_sum(early, core)
    rows_of = early.shape[0] // 2
    grad_up_own = jnp.concatenate(to_row_owners(early[:rows_of], depth, high, core), axis=1)
    grad_down_own = to_block_owners(early[rows_of:])

    dense_spread = lax.dot_general(
        dense_slice, LATE_HALF, (((0,), (0,)), ((), ())), preferred_element_type=jnp.float32
    ).astype(jnp.bfloat16)
    grad_heads = dot(cot, dense_spread).astype(jnp.bfloat16)
    attended, grad_query, grad_key_value = attend(
        order, flips, ends, source, positions.reshape(1, -1), queries, grad_heads, key_all
    )
    attended = attended.astype(jnp.bfloat16)
    attn_part = outer_sum(attended, dense_slice)
    wide_input = hidden.astype(jnp.float32)
    layer_out = wide_input + scattered_tokens(attn_part + mlp_part) + (dense_bias_all + down_bias_all)
    grad_dense = dot(attended, cot)
    grad_second = scattered_tokens(second_part)
    grad_own = scattered_keys(grad_key_value)

    grad_joined = jnp.concatenate([grad_query, grad_own], axis=1)
    grad_mixed = (
        grad_joined.astype(jnp.float32) * cosine - dot(grad_joined, PARTNER) * sine
    ).astype(jnp.bfloat16)
    first_part = times_transposed(grad_mixed, spread_weight[:, :D])
    grad_first = scattered_tokens(first_part)
    grad_qkv = outer_sum(first_in, grad_mixed)
    mixed_sum = jnp.sum(grad_mixed.astype(jnp.float32), axis=0)

    def natural(lanes):
        by_head = lanes.reshape(*lanes.shape[:-1], 2 * OWN, 2, HEAD)
        parts = [by_head[..., :OWN, 0, :], by_head[..., OWN:, 0, :], by_head[..., OWN:, 1, :]]
        return jnp.concatenate([p.reshape(*lanes.shape[:-1], WIDE) for p in parts], axis=-1)

    qkv_bias_rows = natural(mixed_sum).reshape(3, WIDE).T.reshape(32, -1)
    by_row = [
        bias_grad,
        jnp.sum(first_part * normed, axis=0),
        jnp.sum(first_part, axis=0),
        jnp.sum(second_part * normed, axis=0),
        jnp.sum(second_part, axis=0),
    ]
    line = jnp.concatenate([v.reshape(32, -1) for v in by_row] + [qkv_bias_rows, grad_up_bias.reshape(32, -1)], axis=1)
    line = jnp.pad(line, ((0, 0), (0, D - line.shape[1])))
    late = jnp.concatenate(
        [grad_qkv.reshape(32, -1, D), grad_dense.reshape(32, -1, D), line[:, None], jnp.zeros((32, 1, D), jnp.float32)],
        axis=1,
    )
    late = plane_sum(late, core)
    rows_of = D // 32
    dense_of = WIDE // 32
    line = late[rows_of + dense_of]
    row_values = line[: 5 * rows_of].reshape(5, rows_of).T
    at = 5 * rows_of + 3 * dense_of
    block_values = jnp.pad(line[5 * rows_of : at + rows_of], (0, D - 3 * dense_of - rows_of))
    row_part = jnp.concatenate(
        [natural(late[:rows_of]), row_values, jnp.zeros((rows_of, 59), jnp.float32)], axis=1
    )
    got = to_row_owners(row_part, depth, high, core)
    own_rows = got[0].shape[0]
    grad_qkv_own = jnp.stack([g[:, : 3 * WIDE].reshape(own_rows, 3, WIDE) for g in got], axis=2)
    grad_qkv_own = grad_qkv_own.reshape(own_rows, 3 * D)
    values = [g[:, 3 * WIDE : 3 * WIDE + 5] for g in got]
    summed = values[0] + values[1] + values[2] + values[3]
    block_part = to_block_owners(
        jnp.concatenate([late[rows_of : rows_of + dense_of], block_values[None], jnp.zeros((1, D), jnp.float32)])
    )
    grad_dense_own = block_part[:dense_of]
    block_line = block_part[dense_of]
    qkv_bias_own = block_line[: 3 * dense_of].reshape(dense_of, 3)
    up_bias_own = block_line[3 * dense_of : 3 * dense_of + rows_of]
    bias_own = values[0][:, 0]

    own_normed, own_inverse = norm_parts(wide_input)
    input_grad = (
        cotangent.astype(jnp.float32)
        + norm_backward(grad_first, own_normed, own_inverse, attn_gain_all)
        + norm_backward(grad_second, own_normed, own_inverse, mlp_gain_all)
    )
    return (
        layer_out.astype(jnp.bfloat16),
        input_grad.astype(jnp.bfloat16),
        grad_qkv_own,
        qkv_bias_own,
        grad_dense_own,
        bias_own,
        grad_up_own,
        up_bias_own,
        grad_down_own,
        bias_own,
        summed[:, 1],
        summed[:, 2],
        summed[:, 3],
        summed[:, 4],
    )


def solution(mesh):
    fine = Mesh(mesh.devices.reshape(SIZES), AXES)
    weight = ("zh", "c")
    matrix, vector, share = P(AXES, None), P(AXES), P(weight, None)
    part = P(weight)
    return jax.shard_map(
        local,
        mesh=fine,
        in_specs=(
            matrix, share, part, share, part, share, part, share, part, part, part, part, part, P(), matrix,
        ),
        out_specs=(
            matrix, matrix, matrix, matrix, matrix, vector, matrix, vector, matrix,
            vector, vector, vector, vector, vector,
        ),
        check_vma=False,
    )
```

```python
import math

import jax
import jax.numpy as jnp
import numpy as np
from jax import lax
from jax.experimental import pallas as pl
from jax.experimental.pallas import tpu as pltpu
from jax.sharding import Mesh, PartitionSpec as P

D = 768
HEADS = 12
HEAD = 64
ROT = 16
GROUP = 4
OWN = HEADS // GROUP
WIDE = D // GROUP
LANES = 128
SUB = 128
BLOCK = 256
SPAN = 4
AXES = ("x", "y", "zl", "zh", "c")
SIZES = (4, 4, 2, 2, 2)
PLANE = ("x", "y", "c")
norm_eps = 1e-05
masked_value = -1e30


def lane_tables():
    spread = np.zeros((3 * WIDE, 2 * D), np.float32)
    partner = np.zeros((D, D), np.float32)
    for head in range(OWN):
        for lane in range(HEAD):
            source = head * HEAD + lane
            swapped = head * HEAD + (lane ^ (ROT // 2))
            q_lane = head * LANES + lane
            k_lane = OWN * LANES + q_lane
            spread[source, q_lane] = 1
            spread[WIDE + source, k_lane] = 1
            spread[2 * WIDE + source, k_lane + HEAD] = 1
            if lane < ROT:
                spread[swapped, D + q_lane] = 1
                spread[WIDE + swapped, D + k_lane] = 1
                partner[q_lane ^ (ROT // 2), q_lane] = 1
                partner[k_lane ^ (ROT // 2), k_lane] = 1
    padded = np.zeros((D, D // 6 * 8), np.float32)
    for row in range(D):
        padded[row, row // 6 * 8 + row % 6] = 1
    late_half = np.zeros((WIDE, OWN * LANES), np.float32)
    for head in range(OWN):
        for lane in range(HEAD):
            late_half[head * HEAD + lane, head * LANES + HEAD + lane] = 1
    return tuple(t.astype(jnp.bfloat16) for t in (spread, partner[:LANES, :LANES], late_half, padded))


SPREAD, PARTNER, LATE_HALF, PADDED = lane_tables()
SPREAD_QUERIES = np.concatenate([SPREAD[:WIDE, : D // 2], SPREAD[:WIDE, D : D + D // 2]], axis=1)
SPREAD_KEYS = np.concatenate([SPREAD[WIDE:, D // 2 : D], SPREAD[WIDE:, D + D // 2 :]], axis=1)


def dot(a, b):
    return jnp.dot(a, b, preferred_element_type=jnp.float32)


def outer_sum(a, b):
    return lax.dot_general(a, b, (((0,), (0,)), ((), ())), preferred_element_type=jnp.float32)


def times_transposed(a, b):
    return lax.dot_general(a, b, (((1,), (1,)), ((), ())), preferred_element_type=jnp.float32)


def attend_head(
    order, flips, ends, source, side, q_pos, q_in, g_in, kv, out, dq, kept, sent,
    q_rows, q_cols, g_rows, g_cols, col_pos, dq_sum,
):
    core = side[0]
    subs = kv.shape[0]
    blocks = subs // 2
    lanes = q_in.shape[0]
    keys = SPAN * BLOCK
    last_span = [ends[s] // SPAN for s in range(4)]

    def places(span):
        for i in range(SPAN):
            at = order[span * SPAN + i]
            yield at
            yield at + 4

    def load(span):
        return jnp.concatenate([kv[at] for at in places(span)], axis=0)

    def load_turned(span, first):
        return jnp.concatenate([kv[at].T[first : first + HEAD] for at in places(span)], axis=1)

    for s in range(4):
        rows = pl.ds(pl.multiple_of(source[s] * SUB, SUB), SUB)
        here = slice(s * SUB, (s + 1) * SUB)
        q_rows[here] = q_in[rows]
        g_rows[here] = g_in[rows]
        q_cols[:, here] = q_in[rows].T
        g_cols[:, here] = g_in[rows].T
        col_pos[:, here] = q_pos[:, rows]

    def visible(span, first):
        row = lax.broadcasted_iota(jnp.int32, (BLOCK, 1), 0)
        core, member, within = row // SUB, row % SUB // HEAD, row % HEAD
        parts = []
        for i in range(SPAN):
            block = span * SPAN + i
            flip = flips[block]
            piece = 2 * (member + flip - 2 * flip * member) + core
            parts.append(block * BLOCK + piece * HEAD + within)
        return jnp.concatenate(parts, axis=0) <= col_pos[:, first:]

    def regions(make, carry):
        done = 0
        for s in range(4):
            first = s * SUB
            state = tuple(c[:, first:] for c in carry)
            state = lax.fori_loop(done, last_span[s], make(first, False), state)
            state = lax.fori_loop(jnp.maximum(done, last_span[s]), last_span[s] + 1, make(first, True), state)
            done = last_span[s] + 1
            carry = tuple(jnp.concatenate([c[:, :first], n], axis=1) if first else n for c, n in zip(carry, state))
        return carry

    def forward(first, masked):
        def step(span, carry):
            top, total, acc = carry
            scores = dot(load(span), q_cols[:, first:])
            if masked:
                scores = jnp.where(visible(span, first), scores, masked_value)
            new_top = jnp.maximum(top, jnp.max(scores, axis=0, keepdims=True))
            weights = jnp.exp(scores - new_top)
            low = weights.astype(jnp.bfloat16)
            factor = jnp.exp(top - new_top)
            total = total * factor + jnp.sum(weights, axis=0, keepdims=True)
            acc = acc * factor + dot(load_turned(span, HEAD), low)
            return new_top, total, acc

        return step

    top, total, acc = regions(
        forward,
        (
            jnp.full((1, lanes), masked_value, jnp.float32),
            jnp.zeros((1, lanes), jnp.float32),
            jnp.zeros((HEAD, lanes), jnp.float32),
        ),
    )
    attended = acc / total
    log_total = top + jnp.log(total)
    delta = jnp.sum(attended * g_cols[HEAD:].astype(jnp.float32), axis=0, keepdims=True)
    dq_sum[...] = jnp.zeros_like(dq_sum)

    def backward(first, masked):
        def step(span, carry):
            key_value = load(span)
            scores = dot(key_value, q_cols[:, first:])
            probs = jnp.exp(scores - log_total[:, first:])
            if masked:
                probs = jnp.where(visible(span, first), probs, 0.0)
            grad_probs = dot(key_value, g_cols[:, first:])
            grad_scores = (probs * (grad_probs - delta[:, first:])).astype(jnp.bfloat16)
            both = dot(grad_scores, q_rows[first:]) + dot(probs.astype(jnp.bfloat16), g_rows[first:])
            store(span, both.astype(kept.dtype))
            dq_sum[:HEAD, first:] += dot(load_turned(span, 0), grad_scores)
            return carry

        return step

    def store(span, both):
        for i in range(SPAN):
            at = order[span * SPAN + i]
            at = at // 8 * 4 + at % 4
            a, b = both[2 * i * SUB : (2 * i + 1) * SUB], both[(2 * i + 1) * SUB : (2 * i + 2) * SUB]
            kept[at] = jnp.where(core == 0, a, b)
            sent[at] = jnp.where(core == 0, b, a)

    regions(backward, ())

    def clear(span, carry):
        store(span, jnp.zeros((keys, 2 * HEAD), kept.dtype))
        return carry

    lax.fori_loop(last_span[3] + 1, blocks // SPAN, clear, 0)
    for s in range(4):
        rows = pl.ds(pl.multiple_of(source[s] * SUB, SUB), SUB)
        here = slice(s * SUB, (s + 1) * SUB)
        out[:, rows] = attended[:, here]
        dq[rows] = (dq_sum[:, here].T * HEAD**-0.5).astype(dq.dtype)


def attend(head, order, flips, ends, source, side, q_pos, queries, grads, kv):
    rows = queries.shape[0]
    subs = kv.shape[0]
    smem = pl.BlockSpec(memory_space=pltpu.SMEM)
    vmem = pl.BlockSpec(memory_space=pltpu.VMEM)
    tokens = pl.BlockSpec((rows, 128), lambda i: (0, head))
    at = head if kv.shape[2] > 128 else 0
    half = jax.ShapeDtypeStruct((subs // 2, SUB, 128), jnp.bfloat16)
    return pl.pallas_call(
        attend_head,
        grid=(1,),
        out_shape=(
            jax.ShapeDtypeStruct((HEAD, rows), jnp.float32),
            jax.ShapeDtypeStruct((rows, 128), jnp.bfloat16),
            half,
            half,
        ),
        in_specs=[smem] * 5
        + [vmem, tokens, tokens, pl.BlockSpec((subs, SUB, 128), lambda i: (0, 0, at))],
        out_specs=(vmem, vmem, vmem, vmem),
        scratch_shapes=[
            pltpu.VMEM((rows, 128), jnp.bfloat16),
            pltpu.VMEM((128, rows), jnp.bfloat16),
            pltpu.VMEM((rows, 128), jnp.bfloat16),
            pltpu.VMEM((128, rows), jnp.bfloat16),
            pltpu.VMEM((1, rows), jnp.int32),
            pltpu.VMEM((128, rows), jnp.float32),
        ],
        cost_estimate=pl.CostEstimate(flops=30 * 10**9, bytes_accessed=2 * kv.size, transcendentals=0),
        compiler_params=pltpu.CompilerParams(vmem_limit_bytes=50 * 1024 * 1024),
    )(order, flips, ends, source, side, q_pos, queries, grads, kv)


def norm_parts(values):
    center = jnp.mean(values, axis=-1, keepdims=True)
    centered = values - center
    spread = jnp.mean(centered * centered, axis=-1, keepdims=True)
    inverse = lax.rsqrt(spread + norm_eps)
    return centered * inverse, inverse


def norm_backward(grad_out, normed, inverse, norm_gain):
    scaled = grad_out * norm_gain
    return inverse * (
        scaled
        - jnp.mean(scaled, axis=-1, keepdims=True)
        - normed * jnp.mean(scaled * normed, axis=-1, keepdims=True)
    )


def shifted(a, step):
    def target(zl, zh):
        there = (2 * zh + zl + step) % 4
        return (there % 2, there // 2)

    return moved(a, ("zl", "zh"), target)


def other_core(a):
    return lax.ppermute(a, "c", [(0, 1), (1, 0)])


def other_high(a):
    return lax.ppermute(a, "zh", [(0, 1), (1, 0)])


def moved(a, names, target):
    sizes = [SIZES[AXES.index(n)] for n in names]
    pairs = []
    for index in range(int(np.prod(sizes))):
        there = target(*np.unravel_index(index, sizes))
        pairs.append((index, int(np.ravel_multi_index(there, sizes))))
    return lax.ppermute(a, names, pairs)


def in_order(parts, high, low):
    a, b, c, d = parts
    a, b = jnp.where(low == 0, a, b), jnp.where(low == 0, b, a)
    c, d = jnp.where(low == 0, c, d), jnp.where(low == 0, d, c)
    return (
        jnp.where(high == 0, a, c),
        jnp.where(high == 0, b, d),
        jnp.where(high == 0, c, a),
        jnp.where(high == 0, d, b),
    )


def token_rows(parts):
    rows, width = parts[0].shape
    stacked = jnp.stack(parts).reshape(2, 2, 2, rows // 2, width)
    return stacked.transpose(0, 2, 1, 3, 4).reshape(4 * rows, width)


def gathered_tokens(own):
    return token_rows([own, shifted(own, 2), shifted(own, 1), shifted(own, -1)])


def scattered_tokens(total):
    rows, width = total.shape
    parts = total.reshape(2, 2, 2, rows // 8, width).transpose(0, 2, 1, 3, 4).reshape(4, rows // 4, width)
    sent = parts[1:].astype(jnp.bfloat16)
    return (
        parts[0]
        + shifted(sent[0], 2).astype(jnp.float32)
        + shifted(sent[1], -1).astype(jnp.float32)
        + shifted(sent[2], 1).astype(jnp.float32)
    )


def gathered_keys(own):
    whole = lax.all_gather(own, PLANE, axis=0, tiled=True)
    return whole.reshape(-1, SUB, own.shape[1])


def chip_sum(kept, received):
    return (kept.astype(jnp.float32) + received.astype(jnp.float32)).astype(jnp.bfloat16)


def scattered_keys(chip):
    parts = lax.all_to_all(
        chip.reshape(16, -1, chip.shape[-1]), ("x", "y"), split_axis=0, concat_axis=0, tiled=True
    )
    return jnp.sum(parts.astype(jnp.float32), axis=0).astype(jnp.bfloat16)


def padded_rows(a):
    return dot(a, PADDED).astype(jnp.bfloat16)


def row_owner_sums(chunks):
    _, rows, width = chunks.shape
    parts = lax.all_to_all(chunks, AXES, split_axis=0, concat_axis=0, tiled=True)
    return jnp.sum(parts.astype(jnp.float32).reshape(*SIZES, rows, width), axis=(0, 1, 4))


def plane_sum(chunks):
    parts = lax.all_to_all(chunks, PLANE, split_axis=0, concat_axis=0, tiled=True)
    return jnp.sum(parts.astype(jnp.float32), axis=0)


def to_row_owners(rows, slice_index, high, core):
    pieces = rows.reshape(GROUP, -1, rows.shape[1])
    got = []
    for j in range(GROUP):
        piece = lax.dynamic_index_in_dim(pieces, jnp.bitwise_xor(j, slice_index), 0, keepdims=False)

        def target(zl, zh, c, j=j):
            k = j ^ (2 * zh + zl)
            return (c, k // 2, k % 2)

        got.append(moved(piece, ("zl", "zh", "c"), target))
    return in_order(got, high, core)


def to_block_owners(block):
    return moved(block, AXES, lambda x, y, zl, zh, c: (2 * zh + zl, x, y // 2, y % 2, c))


def local(
    hidden,
    qkv_weight,
    qkv_bias,
    dense_weight,
    dense_bias,
    up_weight,
    up_bias,
    down_weight,
    down_bias,
    attn_gain,
    attn_shift,
    mlp_gain,
    mlp_shift,
    block_table,
    cotangent,
):
    x, y, low, high, core = (lax.axis_index(a) for a in AXES)
    depth = 2 * high + low
    tok_rows = hidden.shape[0]
    half_rows = tok_rows // 2
    own_slice = core == low

    tokens = gathered_tokens(hidden)
    cot = gathered_tokens(cotangent)

    theirs = 2 * (1 - high) + low

    sent_columns = []

    def by_group(matrix, starts, width):
        def columns(index):
            parts = [lax.dynamic_slice_in_dim(matrix, at + index * width, width, 1) for at in starts]
            return jnp.concatenate(parts, axis=1)

        kept, sent = columns(depth), columns(theirs)
        sent_columns.append(sent)
        swapped = moved(sent, ("zh", "c"), lambda zh, c: (1 - zh, 1 - c))
        parts = [kept, other_core(kept), other_high(sent), swapped]
        return jnp.concatenate(in_order(parts, high, core), axis=0)

    key_slice = by_group(qkv_weight, (D, 2 * D), WIDE)
    query_slice = by_group(qkv_weight, (0,), WIDE)
    up_slice = by_group(up_weight, (0,), D)
    shards = jnp.concatenate([down_weight, dense_weight], axis=0)
    shards = jnp.where(own_slice, shards, other_core(shards))
    down_slice, dense_slice = shards[:D], shards[D:]

    tokens, qkv_bias, up_bias, dense_bias, down_bias, attn_gain, attn_shift, mlp_gain, mlp_shift = (
        lax.optimization_barrier(
            (tokens, qkv_bias, up_bias, dense_bias, down_bias, attn_gain, attn_shift, mlp_gain, mlp_shift)
        )
    )
    small = jnp.concatenate(
        [qkv_bias, up_bias, dense_bias, down_bias, attn_gain, attn_shift, mlp_gain, mlp_shift]
    ).reshape(1, -1)
    from_core = other_core(small)
    from_high = other_high(small)
    from_both = moved(small, ("zh", "c"), lambda zh, c: (1 - zh, 1 - c))
    small_all = jnp.concatenate(in_order([small, from_core, from_high, from_both], high, core), axis=0)
    small_all = small_all.astype(jnp.float32)
    up_at = 3 * WIDE
    up_bias_slice = jnp.where(own_slice, small, from_core)[0, up_at : up_at + D].astype(jnp.float32)
    qkv_bias_all = small_all[:, : 3 * WIDE].reshape(3, GROUP, WIDE)
    qkv_bias_slice = lax.dynamic_index_in_dim(qkv_bias_all, depth, 1, keepdims=False).reshape(1, -1)
    vectors = [small_all[:, at : at + WIDE].reshape(D) for at in range(up_at + D, small.shape[1], WIDE)]
    dense_bias_all, down_bias_all, attn_gain_all, attn_shift_all, mlp_gain_all, mlp_shift_all = vectors

    block_table = lax.optimization_barrier((block_table, sent_columns[0]))[0]
    members = [depth, (depth + 2) % 4, (depth + 3) % 4, (depth + 1) % 4]
    piece = 2 * (jnp.stack(members).reshape(2, 2) // 2) + core
    ctx = x * 8 + y * 2 + jnp.stack([low, 1 - low])
    own_blocks = block_table[ctx]
    positions = (
        own_blocks[:, :, None, None] * BLOCK
        + piece[:, None, :, None] * half_rows
        + jnp.arange(half_rows, dtype=jnp.int32)
    ).reshape(-1)
    flat = block_table.reshape(-1)
    count = flat.shape[0]
    ids = jnp.arange(count, dtype=jnp.int32)
    place = jnp.sum(jnp.where(flat[None, :] == ids[:, None], ids[None, :], 0), axis=1)
    pair = jnp.bitwise_xor((place // 2) % 2, low)
    order = (place // 4) * 8 + pair * 2 + place % 2
    flips = jnp.where(pair == 0, members[0] // 2, members[2] // 2)
    first = jnp.where(own_blocks[0, 0] < own_blocks[1, 0], 0, 1)
    ends = jnp.sort(own_blocks.reshape(-1))
    source = jnp.stack([2 * first, 2 - 2 * first, 3 - 2 * first, 2 * first + 1]).astype(jnp.int32)
    rotary = 10000.0 ** (-np.arange(0, ROT, 2, dtype=np.float64) / ROT)
    frequency = np.zeros((1, LANES), np.float32)
    frequency[0, :ROT] = np.concatenate([rotary, rotary])
    sign = np.zeros((1, LANES), np.float32)
    sign[0, :ROT] = np.repeat([-1.0, 1.0], ROT // 2)
    angles = positions.astype(jnp.float32)[:, None] * frequency
    cosine = jnp.cos(angles)
    sine = jnp.sin(angles) * sign

    normed, _ = norm_parts(tokens.astype(jnp.float32))
    first_in = (normed * attn_gain_all + attn_shift_all).astype(jnp.bfloat16)
    second_in = (normed * mlp_gain_all + mlp_shift_all).astype(jnp.bfloat16)
    qkv_bias_slice = qkv_bias_slice.astype(jnp.bfloat16)

    def projection(weight, bias, spread):
        weight = dot(weight, spread).astype(jnp.bfloat16)
        projected = dot(first_in, weight) + dot(bias, spread)
        lanes = OWN * LANES
        turned = [
            projected[:, at : at + LANES] * cosine + projected[:, lanes + at : lanes + at + LANES] * sine
            for at in range(0, lanes, LANES)
        ]
        return jnp.concatenate(turned, axis=1), weight[:, :lanes]

    key_value, key_weight = projection(key_slice, qkv_bias_slice[:, WIDE:], SPREAD_KEYS)
    key_value = key_value.astype(jnp.bfloat16)
    key_all = gathered_keys(key_value)
    queries, query_weight = projection(query_slice, qkv_bias_slice[:, :WIDE], SPREAD_QUERIES)
    queries = (queries * HEAD**-0.5).astype(jnp.bfloat16)
    spread_weight = jnp.concatenate([query_weight, key_weight], axis=1)

    pre_act = dot(second_in, up_slice) + up_bias_slice
    cdf_part = 0.5 * (1.0 + lax.erf(pre_act * (1.0 / math.sqrt(2.0))))
    density = jnp.exp(-0.5 * pre_act * pre_act) * (1.0 / math.sqrt(2.0 * math.pi))
    activated = (pre_act * cdf_part).astype(jnp.bfloat16)
    grad_act = times_transposed(cot, down_slice)
    grad_pre_wide = grad_act * (cdf_part + pre_act * density)
    grad_pre = grad_pre_wide.astype(jnp.bfloat16)
    grad_up = outer_sum(second_in, grad_pre).astype(jnp.bfloat16).reshape(32, -1, D)
    grad_down = outer_sum(activated, cot).astype(jnp.bfloat16).reshape(32, -1, D)
    grad_up_bias = jnp.sum(grad_pre.astype(jnp.float32), axis=0)
    second_part = times_transposed(grad_pre, up_slice)
    mlp_part = dot(activated, down_slice)
    second_sums = [jnp.sum(second_part * normed, axis=0), jnp.sum(second_part, axis=0)]
    bias_grad = jnp.sum(cot.astype(jnp.float32), axis=0)

    dense_spread = lax.dot_general(
        dense_slice, LATE_HALF, (((0,), (0,)), ((), ())), preferred_element_type=jnp.float32
    ).astype(jnp.bfloat16)
    grad_heads = dot(cot, dense_spread).astype(jnp.bfloat16)
    queries, grad_heads, grad_up, grad_down, second_part, mlp_part = lax.optimization_barrier(
        (queries, grad_heads, grad_up, grad_down, second_part, mlp_part)
    )
    up_sum = plane_sum(grad_up)
    queries, up_sum, grad_down, key_all = lax.optimization_barrier((queries, up_sum, grad_down, key_all))
    down_sum = plane_sum(grad_down)
    grad_second = scattered_tokens(second_part)
    side = core.reshape(1).astype(jnp.int32)

    def one_head(head, queries):
        return attend(
            head, order, flips, ends, source, side, positions.reshape(1, -1), queries, grad_heads, key_all
        )

    out0, query0, kept0, sent0 = one_head(0, queries)
    queries, out0, down_sum = lax.optimization_barrier((queries, out0, down_sum))
    out1, query1, kept1, sent1 = one_head(1, queries)
    chip0 = chip_sum(kept0, other_core(sent0))
    queries, out1, chip0 = lax.optimization_barrier((queries, out1, chip0))
    out2, query2, kept2, sent2 = one_head(2, queries)
    key0 = scattered_keys(chip0)
    chip1 = chip_sum(kept1, other_core(sent1))
    sent2, chip1, key0 = lax.optimization_barrier((sent2, chip1, key0))
    chip2 = chip_sum(kept2, other_core(sent2))
    key1 = scattered_keys(chip1)
    chip2, key1 = lax.optimization_barrier((chip2, key1))
    key2 = scattered_keys(chip2)
    attended = [o.astype(jnp.bfloat16) for o in (out0, out1, out2)]
    query_grads, key_grads = [query0, query1, query2], [key0, key1, key2]
    attended = jnp.concatenate(attended, axis=0)
    wide_input = hidden.astype(jnp.float32)
    attn_part = outer_sum(attended, dense_slice)
    layer_out = wide_input + scattered_tokens(attn_part + mlp_part) + (dense_bias_all + down_bias_all)
    padded_attended = dot(PADDED[:WIDE, : WIDE // 6 * 8].T, attended).astype(jnp.bfloat16)
    grad_dense = dot(padded_attended, cot).reshape(32, -1, D)
    line = jnp.pad(grad_up_bias.reshape(32, 1, -1), ((0, 0), (6, 1), (0, D - D // 32)))
    block_sums = to_block_owners(plane_sum((grad_dense + line).astype(jnp.bfloat16)))
    grad_dense_own = block_sums[:6]
    up_bias_own = block_sums[6, : D // 32]

    def turned_back(grad):
        return (
            grad.astype(jnp.float32) * cosine - dot(grad, PARTNER) * sine
        ).astype(jnp.bfloat16)

    padded_in = padded_rows(first_in)
    early = jnp.concatenate([turned_back(g) for g in query_grads + key_grads[:-1]], axis=1)
    early_lanes = early.shape[1]
    early_part = times_transposed(early, spread_weight[:, :early_lanes])
    late = turned_back(key_grads[-1])
    first_part = early_part + times_transposed(late, spread_weight[:, early_lanes:D])
    grad_first = scattered_tokens(first_part)

    def natural(lanes):
        by_head = lanes.reshape(*lanes.shape[:-1], 2 * OWN, 2, HEAD)
        parts = [by_head[..., :OWN, 0, :], by_head[..., OWN:, 0, :], by_head[..., OWN:, 1, :]]
        return jnp.stack([p.reshape(*lanes.shape[:-1], WIDE) for p in parts], axis=-2)

    mixed_sum = jnp.concatenate([jnp.sum(g.astype(jnp.float32), axis=0) for g in (early, late)])
    bias_line = lax.dynamic_update_slice_in_dim(
        jnp.zeros((LANES, 18), jnp.float32), natural(mixed_sum).T.reshape(32, 18), 32 * depth, 0
    )
    by_row = [bias_grad, jnp.sum(first_part * normed, axis=0), jnp.sum(first_part, axis=0)] + second_sums
    row_line = jnp.concatenate([v.reshape(-1, 6) for v in by_row], axis=1)
    lines = jnp.stack([jnp.pad(l, ((0, 0), (0, D - l.shape[1]))) for l in (bias_line, row_line)], axis=1)
    grad_qkv = outer_sum(padded_in, jnp.concatenate([early, late], axis=1)).reshape(-1, 8, D)
    grad_qkv = grad_qkv + jnp.pad(lines, ((0, 0), (6, 0), (0, 0)))
    sums = row_owner_sums(grad_qkv.astype(jnp.bfloat16))
    grad_qkv_own = natural(sums[:, :, :6]).transpose(2, 3, 1, 0, 4).reshape(6, 3 * D)
    qkv_bias_own = jnp.sum(sums[:, :, 6, :18], axis=(0, 1)).reshape(6, 3)
    bias_own = sums[0, 0, 7, :6]
    row_values = jnp.sum(sums[:, :, 7, 6:30], axis=(0, 1)).reshape(4, 6)
    attn_gain_own, attn_shift_own, mlp_gain_own, mlp_shift_own = (row_values[i] for i in range(4))
    grad_up_own = jnp.concatenate(to_row_owners(up_sum, depth, high, core), axis=1)
    grad_down_own = to_block_owners(down_sum)

    own_normed, own_inverse = norm_parts(wide_input)
    input_grad = (
        cotangent.astype(jnp.float32)
        + norm_backward(grad_first, own_normed, own_inverse, attn_gain_all)
        + norm_backward(grad_second, own_normed, own_inverse, mlp_gain_all)
    )
    return (
        layer_out.astype(jnp.bfloat16),
        input_grad.astype(jnp.bfloat16),
        grad_qkv_own,
        qkv_bias_own,
        grad_dense_own,
        bias_own,
        grad_up_own,
        up_bias_own,
        grad_down_own,
        bias_own,
        attn_gain_own,
        attn_shift_own,
        mlp_gain_own,
        mlp_shift_own,
    )


def solution(mesh):
    fine = Mesh(mesh.devices.reshape(SIZES), AXES)
    weight = ("zh", "c")
    matrix, vector, share = P(AXES, None), P(AXES), P(weight, None)
    part = P(weight)
    return jax.shard_map(
        local,
        mesh=fine,
        in_specs=(
            matrix, share, part, share, part, share, part, share, part, part, part, part, part, P(), matrix,
        ),
        out_specs=(
            matrix, matrix, matrix, matrix, matrix, vector, matrix, vector, matrix,
            vector, vector, vector, vector, vector,
        ),
        check_vma=False,
    )
```

```python
import math

import jax
import jax.numpy as jnp
import numpy as np
from jax import lax
from jax.experimental import pallas as pl
from jax.experimental.pallas import tpu as pltpu
from jax.sharding import Mesh, PartitionSpec as P

D = 768
HEADS = 12
HEAD = 64
ROT = 16
GROUP = 4
OWN = HEADS // GROUP
WIDE = D // GROUP
LANES = 128
SUB = 128
BLOCK = 256
SPAN = 4
AXES = ("x", "y", "zl", "zh", "c")
SIZES = (4, 4, 2, 2, 2)
PLANE = ("x", "y", "c")
norm_eps = 1e-05
masked_value = -1e30


def lane_tables():
    spread = np.zeros((3 * WIDE, 2 * D), np.float32)
    partner = np.zeros((D, D), np.float32)
    for head in range(OWN):
        for lane in range(HEAD):
            source = head * HEAD + lane
            swapped = head * HEAD + (lane ^ (ROT // 2))
            q_lane = head * LANES + lane
            k_lane = OWN * LANES + q_lane
            spread[source, q_lane] = 1
            spread[WIDE + source, k_lane] = 1
            spread[2 * WIDE + source, k_lane + HEAD] = 1
            if lane < ROT:
                spread[swapped, D + q_lane] = 1
                spread[WIDE + swapped, D + k_lane] = 1
                partner[q_lane ^ (ROT // 2), q_lane] = 1
                partner[k_lane ^ (ROT // 2), k_lane] = 1
    padded = np.zeros((D, D // 6 * 8), np.float32)
    for row in range(D):
        padded[row, row // 6 * 8 + row % 6] = 1
    late_half = np.zeros((WIDE, OWN * LANES), np.float32)
    for head in range(OWN):
        for lane in range(HEAD):
            late_half[head * HEAD + lane, head * LANES + HEAD + lane] = 1
    return tuple(t.astype(jnp.bfloat16) for t in (spread, partner[:LANES, :LANES], late_half, padded))


SPREAD, PARTNER, LATE_HALF, PADDED = lane_tables()
SPREAD_QUERIES = np.concatenate([SPREAD[:WIDE, : D // 2], SPREAD[:WIDE, D : D + D // 2]], axis=1)
SPREAD_KEYS = np.concatenate([SPREAD[WIDE:, D // 2 : D], SPREAD[WIDE:, D + D // 2 :]], axis=1)


def dot(a, b):
    return jnp.dot(a, b, preferred_element_type=jnp.float32)


def outer_sum(a, b):
    return lax.dot_general(a, b, (((0,), (0,)), ((), ())), preferred_element_type=jnp.float32)


def times_transposed(a, b):
    return lax.dot_general(a, b, (((1,), (1,)), ((), ())), preferred_element_type=jnp.float32)


def attend_head(
    order, flips, ends, source, side, q_pos, q_in, g_in, kv, out, dq, kept, sent,
    q_rows, q_cols, g_rows, g_cols, col_pos, dq_sum,
):
    core = side[0]
    subs = kv.shape[0]
    blocks = subs // 2
    lanes = q_in.shape[0]
    keys = SPAN * BLOCK
    last_span = [ends[s] // SPAN for s in range(4)]

    def places(span):
        for i in range(SPAN):
            at = order[span * SPAN + i]
            yield at
            yield at + 4

    def load(span):
        return jnp.concatenate([kv[at] for at in places(span)], axis=0)

    def load_turned(span, first):
        return jnp.concatenate([kv[at].T[first : first + HEAD] for at in places(span)], axis=1)

    for s in range(4):
        rows = pl.ds(pl.multiple_of(source[s] * SUB, SUB), SUB)
        here = slice(s * SUB, (s + 1) * SUB)
        q_rows[here] = q_in[rows]
        g_rows[here] = g_in[rows]
        q_cols[:, here] = q_in[rows].T
        g_cols[:, here] = g_in[rows].T
        col_pos[:, here] = q_pos[:, rows]

    def visible(span, first):
        row = lax.broadcasted_iota(jnp.int32, (BLOCK, 1), 0)
        core, member, within = row // SUB, row % SUB // HEAD, row % HEAD
        parts = []
        for i in range(SPAN):
            block = span * SPAN + i
            flip = flips[block]
            piece = 2 * (member + flip - 2 * flip * member) + core
            parts.append(block * BLOCK + piece * HEAD + within)
        return jnp.concatenate(parts, axis=0) <= col_pos[:, first:]

    def regions(make, carry):
        done = 0
        for s in range(4):
            first = s * SUB
            state = tuple(c[:, first:] for c in carry)
            state = lax.fori_loop(done, last_span[s], make(first, False), state)
            state = lax.fori_loop(jnp.maximum(done, last_span[s]), last_span[s] + 1, make(first, True), state)
            done = last_span[s] + 1
            carry = tuple(jnp.concatenate([c[:, :first], n], axis=1) if first else n for c, n in zip(carry, state))
        return carry

    def forward(first, masked):
        def step(span, carry):
            top, total, acc = carry
            scores = dot(load(span), q_cols[:, first:])
            if masked:
                scores = jnp.where(visible(span, first), scores, masked_value)
            new_top = jnp.maximum(top, jnp.max(scores, axis=0, keepdims=True))
            weights = jnp.exp(scores - new_top)
            low = weights.astype(jnp.bfloat16)
            factor = jnp.exp(top - new_top)
            total = total * factor + jnp.sum(weights, axis=0, keepdims=True)
            acc = acc * factor + dot(load_turned(span, HEAD), low)
            return new_top, total, acc

        return step

    top, total, acc = regions(
        forward,
        (
            jnp.full((1, lanes), masked_value, jnp.float32),
            jnp.zeros((1, lanes), jnp.float32),
            jnp.zeros((HEAD, lanes), jnp.float32),
        ),
    )
    attended = acc / total
    log_total = top + jnp.log(total)
    delta = jnp.sum(attended * g_cols[HEAD:].astype(jnp.float32), axis=0, keepdims=True)
    dq_sum[...] = jnp.zeros_like(dq_sum)

    def backward(first, masked):
        def step(span, carry):
            key_value = load(span)
            scores = dot(key_value, q_cols[:, first:])
            probs = jnp.exp(scores - log_total[:, first:])
            if masked:
                probs = jnp.where(visible(span, first), probs, 0.0)
            grad_probs = dot(key_value, g_cols[:, first:])
            grad_scores = (probs * (grad_probs - delta[:, first:])).astype(jnp.bfloat16)
            both = dot(grad_scores, q_rows[first:]) + dot(probs.astype(jnp.bfloat16), g_rows[first:])
            store(span, both.astype(kept.dtype))
            dq_sum[:HEAD, first:] += dot(load_turned(span, 0), grad_scores)
            return carry

        return step

    def store(span, both):
        for i in range(SPAN):
            at = order[span * SPAN + i]
            at = at // 8 * 4 + at % 4
            a, b = both[2 * i * SUB : (2 * i + 1) * SUB], both[(2 * i + 1) * SUB : (2 * i + 2) * SUB]
            kept[at] = jnp.where(core == 0, a, b)
            sent[at] = jnp.where(core == 0, b, a)

    regions(backward, ())

    def clear(span, carry):
        store(span, jnp.zeros((keys, 2 * HEAD), kept.dtype))
        return carry

    lax.fori_loop(last_span[3] + 1, blocks // SPAN, clear, 0)
    for s in range(4):
        rows = pl.ds(pl.multiple_of(source[s] * SUB, SUB), SUB)
        here = slice(s * SUB, (s + 1) * SUB)
        out[:, rows] = attended[:, here]
        dq[rows] = (dq_sum[:, here].T * HEAD**-0.5).astype(dq.dtype)


def attend(head, order, flips, ends, source, side, q_pos, queries, grads, kv):
    rows = queries.shape[0]
    subs = kv.shape[0]
    smem = pl.BlockSpec(memory_space=pltpu.SMEM)
    vmem = pl.BlockSpec(memory_space=pltpu.VMEM)
    tokens = pl.BlockSpec((rows, 128), lambda i: (0, head))
    at = head if kv.shape[2] > 128 else 0
    half = jax.ShapeDtypeStruct((subs // 2, SUB, 128), jnp.bfloat16)
    return pl.pallas_call(
        attend_head,
        grid=(1,),
        out_shape=(
            jax.ShapeDtypeStruct((HEAD, rows), jnp.float32),
            jax.ShapeDtypeStruct((rows, 128), jnp.bfloat16),
            half,
            half,
        ),
        in_specs=[smem] * 5
        + [vmem, tokens, tokens, pl.BlockSpec((subs, SUB, 128), lambda i: (0, 0, at))],
        out_specs=(vmem, vmem, vmem, vmem),
        scratch_shapes=[
            pltpu.VMEM((rows, 128), jnp.bfloat16),
            pltpu.VMEM((128, rows), jnp.bfloat16),
            pltpu.VMEM((rows, 128), jnp.bfloat16),
            pltpu.VMEM((128, rows), jnp.bfloat16),
            pltpu.VMEM((1, rows), jnp.int32),
            pltpu.VMEM((128, rows), jnp.float32),
        ],
        cost_estimate=pl.CostEstimate(flops=30 * 10**9, bytes_accessed=2 * kv.size, transcendentals=0),
        compiler_params=pltpu.CompilerParams(vmem_limit_bytes=50 * 1024 * 1024),
    )(order, flips, ends, source, side, q_pos, queries, grads, kv)


def norm_parts(values):
    center = jnp.mean(values, axis=-1, keepdims=True)
    centered = values - center
    spread = jnp.mean(centered * centered, axis=-1, keepdims=True)
    inverse = lax.rsqrt(spread + norm_eps)
    return centered * inverse, inverse


def norm_backward(grad_out, normed, inverse, norm_gain):
    scaled = grad_out * norm_gain
    return inverse * (
        scaled
        - jnp.mean(scaled, axis=-1, keepdims=True)
        - normed * jnp.mean(scaled * normed, axis=-1, keepdims=True)
    )


def shifted(a, step):
    def target(zl, zh):
        there = (2 * zh + zl + step) % 4
        return (there % 2, there // 2)

    return moved(a, ("zl", "zh"), target)


def other_core(a):
    return lax.ppermute(a, "c", [(0, 1), (1, 0)])


def other_high(a):
    return lax.ppermute(a, "zh", [(0, 1), (1, 0)])


def moved(a, names, target):
    sizes = [SIZES[AXES.index(n)] for n in names]
    pairs = []
    for index in range(int(np.prod(sizes))):
        there = target(*np.unravel_index(index, sizes))
        pairs.append((index, int(np.ravel_multi_index(there, sizes))))
    return lax.ppermute(a, names, pairs)


def in_order(parts, high, low):
    a, b, c, d = parts
    a, b = jnp.where(low == 0, a, b), jnp.where(low == 0, b, a)
    c, d = jnp.where(low == 0, c, d), jnp.where(low == 0, d, c)
    return (
        jnp.where(high == 0, a, c),
        jnp.where(high == 0, b, d),
        jnp.where(high == 0, c, a),
        jnp.where(high == 0, d, b),
    )


def token_rows(parts):
    rows, width = parts[0].shape
    stacked = jnp.stack(parts).reshape(2, 2, 2, rows // 2, width)
    return stacked.transpose(0, 2, 1, 3, 4).reshape(4 * rows, width)


def gathered_tokens(own):
    return token_rows([own, shifted(own, 2), shifted(own, 1), shifted(own, -1)])


def scattered_tokens(total):
    rows, width = total.shape
    parts = total.reshape(2, 2, 2, rows // 8, width).transpose(0, 2, 1, 3, 4).reshape(4, rows // 4, width)
    sent = parts[1:].astype(jnp.bfloat16)
    return (
        parts[0]
        + shifted(sent[0], 2).astype(jnp.float32)
        + shifted(sent[1], -1).astype(jnp.float32)
        + shifted(sent[2], 1).astype(jnp.float32)
    )


def gathered_keys(own):
    whole = lax.all_gather(own, PLANE, axis=0, tiled=True)
    return whole.reshape(-1, SUB, own.shape[1])


def chip_sum(kept, received):
    return (kept.astype(jnp.float32) + received.astype(jnp.float32)).astype(jnp.bfloat16)


def scattered_keys(chip):
    parts = lax.all_to_all(
        chip.reshape(16, -1, chip.shape[-1]), ("x", "y"), split_axis=0, concat_axis=0, tiled=True
    )
    return jnp.sum(parts.astype(jnp.float32), axis=0).astype(jnp.bfloat16)


def padded_rows(a):
    return dot(a, PADDED).astype(jnp.bfloat16)


def row_owner_sums(chunks):
    _, rows, width = chunks.shape
    parts = lax.all_to_all(chunks, AXES, split_axis=0, concat_axis=0, tiled=True)
    return jnp.sum(parts.astype(jnp.float32).reshape(*SIZES, rows, width), axis=(0, 1, 4))


def plane_sum(chunks):
    parts = lax.all_to_all(chunks, PLANE, split_axis=0, concat_axis=0, tiled=True)
    return jnp.sum(parts.astype(jnp.float32), axis=0)


def to_row_owners(rows, slice_index, high, core):
    pieces = rows.reshape(GROUP, -1, rows.shape[1])
    got = []
    for j in range(GROUP):
        piece = lax.dynamic_index_in_dim(pieces, jnp.bitwise_xor(j, slice_index), 0, keepdims=False)

        def target(zl, zh, c, j=j):
            k = j ^ (2 * zh + zl)
            return (c, k // 2, k % 2)

        got.append(moved(piece, ("zl", "zh", "c"), target))
    return in_order(got, high, core)


def to_block_owners(block):
    return moved(block, AXES, lambda x, y, zl, zh, c: (2 * zh + zl, x, y // 2, y % 2, c))


def local(
    hidden,
    qkv_weight,
    qkv_bias,
    dense_weight,
    dense_bias,
    up_weight,
    up_bias,
    down_weight,
    down_bias,
    attn_gain,
    attn_shift,
    mlp_gain,
    mlp_shift,
    block_table,
    cotangent,
):
    x, y, low, high, core = (lax.axis_index(a) for a in AXES)
    depth = 2 * high + low
    tok_rows = hidden.shape[0]
    half_rows = tok_rows // 2
    own_slice = core == low

    tokens = gathered_tokens(hidden)
    cot = gathered_tokens(cotangent)

    theirs = 2 * (1 - high) + low

    sent_columns = []

    def by_group(matrix, starts, width):
        def columns(index):
            parts = [lax.dynamic_slice_in_dim(matrix, at + index * width, width, 1) for at in starts]
            return jnp.concatenate(parts, axis=1)

        kept, sent = columns(depth), columns(theirs)
        sent_columns.append(sent)
        swapped = moved(sent, ("zh", "c"), lambda zh, c: (1 - zh, 1 - c))
        parts = [kept, other_core(kept), other_high(sent), swapped]
        return jnp.concatenate(in_order(parts, high, core), axis=0)

    key_slice = by_group(qkv_weight, (D, 2 * D), WIDE)
    query_slice = by_group(qkv_weight, (0,), WIDE)
    up_slice = by_group(up_weight, (0,), D)
    shards = jnp.concatenate([down_weight, dense_weight], axis=0)
    shards = jnp.where(own_slice, shards, other_core(shards))
    down_slice, dense_slice = shards[:D], shards[D:]

    tokens, qkv_bias, up_bias, dense_bias, down_bias, attn_gain, attn_shift, mlp_gain, mlp_shift = (
        lax.optimization_barrier(
            (tokens, qkv_bias, up_bias, dense_bias, down_bias, attn_gain, attn_shift, mlp_gain, mlp_shift)
        )
    )
    small = jnp.concatenate(
        [qkv_bias, up_bias, dense_bias, down_bias, attn_gain, attn_shift, mlp_gain, mlp_shift]
    ).reshape(1, -1)
    from_core = other_core(small)
    from_high = other_high(small)
    from_both = moved(small, ("zh", "c"), lambda zh, c: (1 - zh, 1 - c))
    small_all = jnp.concatenate(in_order([small, from_core, from_high, from_both], high, core), axis=0)
    small_all = small_all.astype(jnp.float32)
    up_at = 3 * WIDE
    up_bias_slice = jnp.where(own_slice, small, from_core)[0, up_at : up_at + D].astype(jnp.float32)
    qkv_bias_all = small_all[:, : 3 * WIDE].reshape(3, GROUP, WIDE)
    qkv_bias_slice = lax.dynamic_index_in_dim(qkv_bias_all, depth, 1, keepdims=False).reshape(1, -1)
    vectors = [small_all[:, at : at + WIDE].reshape(D) for at in range(up_at + D, small.shape[1], WIDE)]
    dense_bias_all, down_bias_all, attn_gain_all, attn_shift_all, mlp_gain_all, mlp_shift_all = vectors

    block_table = lax.optimization_barrier((block_table, sent_columns[0]))[0]
    members = [depth, (depth + 2) % 4, (depth + 3) % 4, (depth + 1) % 4]
    piece = 2 * (jnp.stack(members).reshape(2, 2) // 2) + core
    ctx = x * 8 + y * 2 + jnp.stack([low, 1 - low])
    own_blocks = block_table[ctx]
    positions = (
        own_blocks[:, :, None, None] * BLOCK
        + piece[:, None, :, None] * half_rows
        + jnp.arange(half_rows, dtype=jnp.int32)
    ).reshape(-1)
    flat = block_table.reshape(-1)
    count = flat.shape[0]
    ids = jnp.arange(count, dtype=jnp.int32)
    place = jnp.sum(jnp.where(flat[None, :] == ids[:, None], ids[None, :], 0), axis=1)
    pair = jnp.bitwise_xor((place // 2) % 2, low)
    order = (place // 4) * 8 + pair * 2 + place % 2
    flips = jnp.where(pair == 0, members[0] // 2, members[2] // 2)
    first = jnp.where(own_blocks[0, 0] < own_blocks[1, 0], 0, 1)
    ends = jnp.sort(own_blocks.reshape(-1))
    source = jnp.stack([2 * first, 2 - 2 * first, 3 - 2 * first, 2 * first + 1]).astype(jnp.int32)
    rotary = 10000.0 ** (-np.arange(0, ROT, 2, dtype=np.float64) / ROT)
    frequency = np.zeros((1, LANES), np.float32)
    frequency[0, :ROT] = np.concatenate([rotary, rotary])
    sign = np.zeros((1, LANES), np.float32)
    sign[0, :ROT] = np.repeat([-1.0, 1.0], ROT // 2)
    angles = positions.astype(jnp.float32)[:, None] * frequency
    cosine = jnp.cos(angles)
    sine = jnp.sin(angles) * sign

    normed, _ = norm_parts(tokens.astype(jnp.float32))
    first_in = (normed * attn_gain_all + attn_shift_all).astype(jnp.bfloat16)
    second_in = (normed * mlp_gain_all + mlp_shift_all).astype(jnp.bfloat16)
    qkv_bias_slice = qkv_bias_slice.astype(jnp.bfloat16)

    def projection(weight, bias, spread):
        weight = dot(weight, spread).astype(jnp.bfloat16)
        projected = dot(first_in, weight) + dot(bias, spread)
        lanes = OWN * LANES
        turned = [
            projected[:, at : at + LANES] * cosine + projected[:, lanes + at : lanes + at + LANES] * sine
            for at in range(0, lanes, LANES)
        ]
        return jnp.concatenate(turned, axis=1), weight[:, :lanes]

    key_value, key_weight = projection(key_slice, qkv_bias_slice[:, WIDE:], SPREAD_KEYS)
    key_value = key_value.astype(jnp.bfloat16)
    key_value, cot, up_slice, shards = lax.optimization_barrier((key_value, cot, up_slice, shards))
    down_slice, dense_slice = shards[:D], shards[D:]
    key_all = gathered_keys(key_value)
    queries, query_weight = projection(query_slice, qkv_bias_slice[:, :WIDE], SPREAD_QUERIES)
    queries = (queries * HEAD**-0.5).astype(jnp.bfloat16)
    spread_weight = jnp.concatenate([query_weight, key_weight], axis=1)

    pre_act = dot(second_in, up_slice) + up_bias_slice
    cdf_part = 0.5 * (1.0 + lax.erf(pre_act * (1.0 / math.sqrt(2.0))))
    density = jnp.exp(-0.5 * pre_act * pre_act) * (1.0 / math.sqrt(2.0 * math.pi))
    activated = (pre_act * cdf_part).astype(jnp.bfloat16)
    grad_act = times_transposed(cot, down_slice)
    grad_pre_wide = grad_act * (cdf_part + pre_act * density)
    grad_pre = grad_pre_wide.astype(jnp.bfloat16)
    grad_up = outer_sum(second_in, grad_pre).astype(jnp.bfloat16).reshape(32, -1, D)
    grad_down = outer_sum(activated, cot).astype(jnp.bfloat16).reshape(32, -1, D)
    grad_up_bias = jnp.sum(grad_pre.astype(jnp.float32), axis=0)
    second_part = times_transposed(grad_pre, up_slice)
    mlp_part = dot(activated, down_slice)
    second_sums = [jnp.sum(second_part * normed, axis=0), jnp.sum(second_part, axis=0)]
    bias_grad = jnp.sum(cot.astype(jnp.float32), axis=0)

    dense_spread = lax.dot_general(
        dense_slice, LATE_HALF, (((0,), (0,)), ((), ())), preferred_element_type=jnp.float32
    ).astype(jnp.bfloat16)
    grad_heads = dot(cot, dense_spread).astype(jnp.bfloat16)
    queries, grad_heads, grad_up, grad_down, second_part, mlp_part = lax.optimization_barrier(
        (queries, grad_heads, grad_up, grad_down, second_part, mlp_part)
    )
    up_sum = plane_sum(grad_up)
    queries, up_sum, grad_down, key_all = lax.optimization_barrier((queries, up_sum, grad_down, key_all))
    down_sum = plane_sum(grad_down)
    grad_second = scattered_tokens(second_part)
    side = core.reshape(1).astype(jnp.int32)

    def one_head(head, queries):
        return attend(
            head, order, flips, ends, source, side, positions.reshape(1, -1), queries, grad_heads, key_all
        )

    out0, query0, kept0, sent0 = one_head(0, queries)
    queries, out0, down_sum = lax.optimization_barrier((queries, out0, down_sum))
    out1, query1, kept1, sent1 = one_head(1, queries)
    chip0 = chip_sum(kept0, other_core(sent0))
    queries, out1, chip0 = lax.optimization_barrier((queries, out1, chip0))
    out2, query2, kept2, sent2 = one_head(2, queries)
    key0 = scattered_keys(chip0)
    chip1 = chip_sum(kept1, other_core(sent1))
    sent2, chip1, key0 = lax.optimization_barrier((sent2, chip1, key0))
    chip2 = chip_sum(kept2, other_core(sent2))
    key1 = scattered_keys(chip1)
    chip2, key1 = lax.optimization_barrier((chip2, key1))
    key2 = scattered_keys(chip2)
    attended = [o.astype(jnp.bfloat16) for o in (out0, out1, out2)]
    query_grads, key_grads = [query0, query1, query2], [key0, key1, key2]
    attended = jnp.concatenate(attended, axis=0)
    wide_input = hidden.astype(jnp.float32)
    attn_part = outer_sum(attended, dense_slice)
    layer_out = wide_input + scattered_tokens(attn_part + mlp_part) + (dense_bias_all + down_bias_all)
    padded_attended = dot(PADDED[:WIDE, : WIDE // 6 * 8].T, attended).astype(jnp.bfloat16)
    grad_dense = dot(padded_attended, cot).reshape(32, -1, D)
    line = jnp.pad(grad_up_bias.reshape(32, 1, -1), ((0, 0), (6, 1), (0, D - D // 32)))
    block_sums = to_block_owners(plane_sum((grad_dense + line).astype(jnp.bfloat16)))
    grad_dense_own = block_sums[:6]
    up_bias_own = block_sums[6, : D // 32]

    def turned_back(grad):
        return (
            grad.astype(jnp.float32) * cosine - dot(grad, PARTNER) * sine
        ).astype(jnp.bfloat16)

    padded_in = padded_rows(first_in)
    early = jnp.concatenate([turned_back(g) for g in query_grads + key_grads[:-1]], axis=1)
    early_lanes = early.shape[1]
    early_part = times_transposed(early, spread_weight[:, :early_lanes])
    early_grad = outer_sum(padded_in, early).astype(jnp.bfloat16).reshape(-1, 8, early_lanes)
    early_part, early_grad, last = lax.optimization_barrier((early_part, early_grad, key_grads[-1]))
    late = turned_back(last)
    first_part = early_part + times_transposed(late, spread_weight[:, early_lanes:D])
    grad_first = scattered_tokens(first_part)

    def natural(lanes):
        by_head = lanes.reshape(*lanes.shape[:-1], 2 * OWN, 2, HEAD)
        parts = [by_head[..., :OWN, 0, :], by_head[..., OWN:, 0, :], by_head[..., OWN:, 1, :]]
        return jnp.stack([p.reshape(*lanes.shape[:-1], WIDE) for p in parts], axis=-2)

    mixed_sum = jnp.concatenate([jnp.sum(g.astype(jnp.float32), axis=0) for g in (early, late)])
    bias_line = lax.dynamic_update_slice_in_dim(
        jnp.zeros((LANES, 18), jnp.float32), natural(mixed_sum).T.reshape(32, 18), 32 * depth, 0
    )
    by_row = [bias_grad, jnp.sum(first_part * normed, axis=0), jnp.sum(first_part, axis=0)] + second_sums
    row_line = jnp.concatenate([v.reshape(-1, 6) for v in by_row], axis=1)
    lines = jnp.stack([jnp.pad(l, ((0, 0), (0, D - l.shape[1]))) for l in (bias_line, row_line)], axis=1)
    late_grad = outer_sum(padded_in, late).astype(jnp.bfloat16).reshape(-1, 8, LANES)
    grad_qkv = jnp.concatenate([early_grad, late_grad], axis=2)
    sums = row_owner_sums(grad_qkv + jnp.pad(lines.astype(jnp.bfloat16), ((0, 0), (6, 0), (0, 0))))
    grad_qkv_own = natural(sums[:, :, :6]).transpose(2, 3, 1, 0, 4).reshape(6, 3 * D)
    qkv_bias_own = jnp.sum(sums[:, :, 6, :18], axis=(0, 1)).reshape(6, 3)
    bias_own = sums[0, 0, 7, :6]
    row_values = jnp.sum(sums[:, :, 7, 6:30], axis=(0, 1)).reshape(4, 6)
    attn_gain_own, attn_shift_own, mlp_gain_own, mlp_shift_own = (row_values[i] for i in range(4))
    grad_up_own = jnp.concatenate(to_row_owners(up_sum, depth, high, core), axis=1)
    grad_down_own = to_block_owners(down_sum)

    own_normed, own_inverse = norm_parts(wide_input)
    input_grad = (
        cotangent.astype(jnp.float32)
        + norm_backward(grad_first, own_normed, own_inverse, attn_gain_all)
        + norm_backward(grad_second, own_normed, own_inverse, mlp_gain_all)
    )
    return (
        layer_out.astype(jnp.bfloat16),
        input_grad.astype(jnp.bfloat16),
        grad_qkv_own,
        qkv_bias_own,
        grad_dense_own,
        bias_own,
        grad_up_own,
        up_bias_own,
        grad_down_own,
        bias_own,
        attn_gain_own,
        attn_shift_own,
        mlp_gain_own,
        mlp_shift_own,
    )


def solution(mesh):
    fine = Mesh(mesh.devices.reshape(SIZES), AXES)
    weight = ("zh", "c")
    matrix, vector, share = P(AXES, None), P(AXES), P(weight, None)
    part = P(weight)
    return jax.shard_map(
        local,
        mesh=fine,
        in_specs=(
            matrix, share, part, share, part, share, part, share, part, part, part, part, part, P(), matrix,
        ),
        out_specs=(
            matrix, matrix, matrix, matrix, matrix, vector, matrix, vector, matrix,
            vector, vector, vector, vector, vector,
        ),
        check_vma=False,
    )
```

```python
import math

import jax
import jax.numpy as jnp
import numpy as np
from jax import lax
from jax.experimental import pallas as pl
from jax.experimental.pallas import tpu as pltpu
from jax.sharding import Mesh, PartitionSpec as P

D = 768
HEADS = 12
HEAD = 64
ROT = 16
GROUP = 4
OWN = HEADS // GROUP
WIDE = D // GROUP
LANES = 128
SUB = 128
BLOCK = 256
SPAN = 4
AXES = ("x", "y", "zl", "zh", "c")
SIZES = (4, 4, 2, 2, 2)
PLANE = ("x", "y", "c")
norm_eps = 1e-05
masked_value = -1e30


def lane_tables():
    spread = np.zeros((3 * WIDE, 2 * D), np.float32)
    partner = np.zeros((D, D), np.float32)
    for head in range(OWN):
        for lane in range(HEAD):
            source = head * HEAD + lane
            swapped = head * HEAD + (lane ^ (ROT // 2))
            q_lane = head * LANES + lane
            k_lane = OWN * LANES + q_lane
            spread[source, q_lane] = 1
            spread[WIDE + source, k_lane] = 1
            spread[2 * WIDE + source, k_lane + HEAD] = 1
            if lane < ROT:
                spread[swapped, D + q_lane] = 1
                spread[WIDE + swapped, D + k_lane] = 1
                partner[q_lane ^ (ROT // 2), q_lane] = 1
                partner[k_lane ^ (ROT // 2), k_lane] = 1
    padded = np.zeros((D, D // 6 * 8), np.float32)
    for row in range(D):
        padded[row, row // 6 * 8 + row % 6] = 1
    late_half = np.zeros((WIDE, OWN * LANES), np.float32)
    for head in range(OWN):
        for lane in range(HEAD):
            late_half[head * HEAD + lane, head * LANES + HEAD + lane] = 1
    return tuple(t.astype(jnp.bfloat16) for t in (spread, partner[:LANES, :LANES], late_half, padded))


SPREAD, PARTNER, LATE_HALF, PADDED = lane_tables()
SPREAD_QUERIES = np.concatenate([SPREAD[:WIDE, : D // 2], SPREAD[:WIDE, D : D + D // 2]], axis=1)
SPREAD_KEYS = np.concatenate([SPREAD[WIDE:, D // 2 : D], SPREAD[WIDE:, D + D // 2 :]], axis=1)


def dot(a, b):
    return jnp.dot(a, b, preferred_element_type=jnp.float32)


def outer_sum(a, b):
    return lax.dot_general(a, b, (((0,), (0,)), ((), ())), preferred_element_type=jnp.float32)


def times_transposed(a, b):
    return lax.dot_general(a, b, (((1,), (1,)), ((), ())), preferred_element_type=jnp.float32)


def attend_head(
    order, flips, ends, source, side, q_pos, q_in, g_in, kv, out, dq, kept, sent,
    q_rows, q_cols, g_rows, g_cols, col_pos, dq_sum,
):
    core = side[0]
    subs = kv.shape[0]
    blocks = subs // 2
    lanes = q_in.shape[0]
    keys = SPAN * BLOCK
    last_span = [ends[s] // SPAN for s in range(4)]

    def places(span):
        for i in range(SPAN):
            at = order[span * SPAN + i]
            yield at
            yield at + 4

    def load(span):
        return jnp.concatenate([kv[at] for at in places(span)], axis=0)

    def load_turned(span, first):
        return jnp.concatenate([kv[at].T[first : first + HEAD] for at in places(span)], axis=1)

    for s in range(4):
        rows = pl.ds(pl.multiple_of(source[s] * SUB, SUB), SUB)
        here = slice(s * SUB, (s + 1) * SUB)
        q_rows[here] = q_in[rows]
        g_rows[here] = g_in[rows]
        q_cols[:, here] = q_in[rows].T
        g_cols[:, here] = g_in[rows].T
        col_pos[:, here] = q_pos[:, rows]

    def visible(span, first):
        row = lax.broadcasted_iota(jnp.int32, (BLOCK, 1), 0)
        core, member, within = row // SUB, row % SUB // HEAD, row % HEAD
        parts = []
        for i in range(SPAN):
            block = span * SPAN + i
            flip = flips[block]
            piece = 2 * (member + flip - 2 * flip * member) + core
            parts.append(block * BLOCK + piece * HEAD + within)
        return jnp.concatenate(parts, axis=0) <= col_pos[:, first:]

    def regions(make, carry):
        done = 0
        for s in range(4):
            first = s * SUB
            state = tuple(c[:, first:] for c in carry)
            state = lax.fori_loop(done, last_span[s], make(first, False), state)
            state = lax.fori_loop(jnp.maximum(done, last_span[s]), last_span[s] + 1, make(first, True), state)
            done = last_span[s] + 1
            carry = tuple(jnp.concatenate([c[:, :first], n], axis=1) if first else n for c, n in zip(carry, state))
        return carry

    def forward(first, masked):
        def step(span, carry):
            top, total, acc = carry
            scores = dot(load(span), q_cols[:, first:])
            if masked:
                scores = jnp.where(visible(span, first), scores, masked_value)
            new_top = jnp.maximum(top, jnp.max(scores, axis=0, keepdims=True))
            weights = jnp.exp(scores - new_top)
            low = weights.astype(jnp.bfloat16)
            factor = jnp.exp(top - new_top)
            total = total * factor + jnp.sum(weights, axis=0, keepdims=True)
            acc = acc * factor + dot(load_turned(span, HEAD), low)
            return new_top, total, acc

        return step

    top, total, acc = regions(
        forward,
        (
            jnp.full((1, lanes), masked_value, jnp.float32),
            jnp.zeros((1, lanes), jnp.float32),
            jnp.zeros((HEAD, lanes), jnp.float32),
        ),
    )
    attended = acc / total
    log_total = top + jnp.log(total)
    delta = jnp.sum(attended * g_cols[HEAD:].astype(jnp.float32), axis=0, keepdims=True)
    dq_sum[...] = jnp.zeros_like(dq_sum)

    def backward(first, masked):
        def step(span, carry):
            key_value = load(span)
            scores = dot(key_value, q_cols[:, first:])
            probs = jnp.exp(scores - log_total[:, first:])
            if masked:
                probs = jnp.where(visible(span, first), probs, 0.0)
            grad_probs = dot(key_value, g_cols[:, first:])
            grad_scores = (probs * (grad_probs - delta[:, first:])).astype(jnp.bfloat16)
            both = dot(grad_scores, q_rows[first:]) + dot(probs.astype(jnp.bfloat16), g_rows[first:])
            store(span, both.astype(kept.dtype))
            dq_sum[:HEAD, first:] += dot(load_turned(span, 0), grad_scores)
            return carry

        return step

    def store(span, both):
        for i in range(SPAN):
            at = order[span * SPAN + i]
            at = at // 8 * 4 + at % 4
            a, b = both[2 * i * SUB : (2 * i + 1) * SUB], both[(2 * i + 1) * SUB : (2 * i + 2) * SUB]
            kept[at] = jnp.where(core == 0, a, b)
            sent[at] = jnp.where(core == 0, b, a)

    regions(backward, ())

    def clear(span, carry):
        store(span, jnp.zeros((keys, 2 * HEAD), kept.dtype))
        return carry

    lax.fori_loop(last_span[3] + 1, blocks // SPAN, clear, 0)
    for s in range(4):
        rows = pl.ds(pl.multiple_of(source[s] * SUB, SUB), SUB)
        here = slice(s * SUB, (s + 1) * SUB)
        out[:, rows] = attended[:, here]
        dq[rows] = (dq_sum[:, here].T * HEAD**-0.5).astype(dq.dtype)


def attend(head, order, flips, ends, source, side, q_pos, queries, grads, kv):
    rows = queries.shape[0]
    subs = kv.shape[0]
    smem = pl.BlockSpec(memory_space=pltpu.SMEM)
    vmem = pl.BlockSpec(memory_space=pltpu.VMEM)
    tokens = pl.BlockSpec((rows, 128), lambda i: (0, head))
    at = head if kv.shape[2] > 128 else 0
    half = jax.ShapeDtypeStruct((subs // 2, SUB, 128), jnp.bfloat16)
    return pl.pallas_call(
        attend_head,
        grid=(1,),
        out_shape=(
            jax.ShapeDtypeStruct((HEAD, rows), jnp.float32),
            jax.ShapeDtypeStruct((rows, 128), jnp.bfloat16),
            half,
            half,
        ),
        in_specs=[smem] * 5
        + [vmem, tokens, tokens, pl.BlockSpec((subs, SUB, 128), lambda i: (0, 0, at))],
        out_specs=(vmem, vmem, vmem, vmem),
        scratch_shapes=[
            pltpu.VMEM((rows, 128), jnp.bfloat16),
            pltpu.VMEM((128, rows), jnp.bfloat16),
            pltpu.VMEM((rows, 128), jnp.bfloat16),
            pltpu.VMEM((128, rows), jnp.bfloat16),
            pltpu.VMEM((1, rows), jnp.int32),
            pltpu.VMEM((128, rows), jnp.float32),
        ],
        cost_estimate=pl.CostEstimate(flops=30 * 10**9, bytes_accessed=2 * kv.size, transcendentals=0),
        compiler_params=pltpu.CompilerParams(vmem_limit_bytes=50 * 1024 * 1024),
    )(order, flips, ends, source, side, q_pos, queries, grads, kv)


def norm_parts(values):
    center = jnp.mean(values, axis=-1, keepdims=True)
    centered = values - center
    spread = jnp.mean(centered * centered, axis=-1, keepdims=True)
    inverse = lax.rsqrt(spread + norm_eps)
    return centered * inverse, inverse


def norm_backward(grad_out, normed, inverse, norm_gain):
    scaled = grad_out * norm_gain
    return inverse * (
        scaled
        - jnp.mean(scaled, axis=-1, keepdims=True)
        - normed * jnp.mean(scaled * normed, axis=-1, keepdims=True)
    )


def shifted(a, step):
    def target(zl, zh):
        there = (2 * zh + zl + step) % 4
        return (there % 2, there // 2)

    return moved(a, ("zl", "zh"), target)


def other_core(a):
    return lax.ppermute(a, "c", [(0, 1), (1, 0)])


def other_high(a):
    return lax.ppermute(a, "zh", [(0, 1), (1, 0)])


def moved(a, names, target):
    sizes = [SIZES[AXES.index(n)] for n in names]
    pairs = []
    for index in range(int(np.prod(sizes))):
        there = target(*np.unravel_index(index, sizes))
        pairs.append((index, int(np.ravel_multi_index(there, sizes))))
    return lax.ppermute(a, names, pairs)


def in_order(parts, high, low):
    a, b, c, d = parts
    a, b = jnp.where(low == 0, a, b), jnp.where(low == 0, b, a)
    c, d = jnp.where(low == 0, c, d), jnp.where(low == 0, d, c)
    return (
        jnp.where(high == 0, a, c),
        jnp.where(high == 0, b, d),
        jnp.where(high == 0, c, a),
        jnp.where(high == 0, d, b),
    )


def token_rows(parts):
    rows, width = parts[0].shape
    stacked = jnp.stack(parts).reshape(2, 2, 2, rows // 2, width)
    return stacked.transpose(0, 2, 1, 3, 4).reshape(4 * rows, width)


def gathered_tokens(own):
    return token_rows([own, shifted(own, 2), shifted(own, 1), shifted(own, -1)])


def scattered_tokens(total):
    rows, width = total.shape
    parts = total.reshape(2, 2, 2, rows // 8, width).transpose(0, 2, 1, 3, 4).reshape(4, rows // 4, width)
    sent = parts[1:].astype(jnp.bfloat16)
    return (
        parts[0]
        + shifted(sent[0], 2).astype(jnp.float32)
        + shifted(sent[1], -1).astype(jnp.float32)
        + shifted(sent[2], 1).astype(jnp.float32)
    )


def gathered_keys(own):
    whole = lax.all_gather(own, PLANE, axis=0, tiled=True)
    return whole.reshape(-1, SUB, own.shape[1])


def chip_sum(kept, received):
    return (kept.astype(jnp.float32) + received.astype(jnp.float32)).astype(jnp.bfloat16)


def scattered_keys(chip):
    parts = lax.all_to_all(
        chip.reshape(16, -1, chip.shape[-1]), ("x", "y"), split_axis=0, concat_axis=0, tiled=True
    )
    return jnp.sum(parts.astype(jnp.float32), axis=0).astype(jnp.bfloat16)


def padded_rows(a):
    return dot(a, PADDED).astype(jnp.bfloat16)


def row_owner_sums(chunks):
    _, rows, width = chunks.shape
    parts = lax.all_to_all(chunks, AXES, split_axis=0, concat_axis=0, tiled=True)
    return jnp.sum(parts.astype(jnp.float32).reshape(*SIZES, rows, width), axis=(0, 1, 4))


def plane_sum(chunks):
    parts = lax.all_to_all(chunks, PLANE, split_axis=0, concat_axis=0, tiled=True)
    return jnp.sum(parts.astype(jnp.float32), axis=0)


def to_row_owners(rows, slice_index, high, core):
    pieces = rows.reshape(GROUP, -1, rows.shape[1])
    got = []
    for j in range(GROUP):
        piece = lax.dynamic_index_in_dim(pieces, jnp.bitwise_xor(j, slice_index), 0, keepdims=False)

        def target(zl, zh, c, j=j):
            k = j ^ (2 * zh + zl)
            return (c, k // 2, k % 2)

        got.append(moved(piece, ("zl", "zh", "c"), target))
    return in_order(got, high, core)


def to_block_owners(block):
    return moved(block, AXES, lambda x, y, zl, zh, c: (2 * zh + zl, x, y // 2, y % 2, c))


def local(
    hidden,
    qkv_weight,
    qkv_bias,
    dense_weight,
    dense_bias,
    up_weight,
    up_bias,
    down_weight,
    down_bias,
    attn_gain,
    attn_shift,
    mlp_gain,
    mlp_shift,
    block_table,
    cotangent,
):
    x, y, low, high, core = (lax.axis_index(a) for a in AXES)
    depth = 2 * high + low
    tok_rows = hidden.shape[0]
    half_rows = tok_rows // 2
    own_slice = core == low

    tokens = gathered_tokens(hidden)
    cot = gathered_tokens(cotangent)

    theirs = 2 * (1 - high) + low

    sent_columns = []

    def by_group(matrix, starts, width):
        def columns(index):
            parts = [lax.dynamic_slice_in_dim(matrix, at + index * width, width, 1) for at in starts]
            return jnp.concatenate(parts, axis=1)

        kept, sent = columns(depth), columns(theirs)
        sent_columns.append(sent)
        swapped = moved(sent, ("zh", "c"), lambda zh, c: (1 - zh, 1 - c))
        parts = [kept, other_core(kept), other_high(sent), swapped]
        return jnp.concatenate(in_order(parts, high, core), axis=0)

    key_slice = by_group(qkv_weight, (D, 2 * D), WIDE)
    query_slice = by_group(qkv_weight, (0,), WIDE)
    up_slice = by_group(up_weight, (0,), D)
    shards = jnp.concatenate([down_weight, dense_weight], axis=0)
    shards = jnp.where(own_slice, shards, other_core(shards))
    down_slice, dense_slice = shards[:D], shards[D:]

    tokens, qkv_bias, up_bias, dense_bias, down_bias, attn_gain, attn_shift, mlp_gain, mlp_shift = (
        lax.optimization_barrier(
            (tokens, qkv_bias, up_bias, dense_bias, down_bias, attn_gain, attn_shift, mlp_gain, mlp_shift)
        )
    )
    small = jnp.concatenate(
        [qkv_bias, up_bias, dense_bias, down_bias, attn_gain, attn_shift, mlp_gain, mlp_shift]
    ).reshape(1, -1)
    from_core = other_core(small)
    from_high = other_high(small)
    from_both = moved(small, ("zh", "c"), lambda zh, c: (1 - zh, 1 - c))
    small_all = jnp.concatenate(in_order([small, from_core, from_high, from_both], high, core), axis=0)
    small_all = small_all.astype(jnp.float32)
    up_at = 3 * WIDE
    up_bias_slice = jnp.where(own_slice, small, from_core)[0, up_at : up_at + D].astype(jnp.float32)
    qkv_bias_all = small_all[:, : 3 * WIDE].reshape(3, GROUP, WIDE)
    qkv_bias_slice = lax.dynamic_index_in_dim(qkv_bias_all, depth, 1, keepdims=False).reshape(1, -1)
    vectors = [small_all[:, at : at + WIDE].reshape(D) for at in range(up_at + D, small.shape[1], WIDE)]
    dense_bias_all, down_bias_all, attn_gain_all, attn_shift_all, mlp_gain_all, mlp_shift_all = vectors

    block_table = lax.optimization_barrier((block_table, sent_columns[0]))[0]
    members = [depth, (depth + 2) % 4, (depth + 3) % 4, (depth + 1) % 4]
    piece = 2 * (jnp.stack(members).reshape(2, 2) // 2) + core
    ctx = x * 8 + y * 2 + jnp.stack([low, 1 - low])
    own_blocks = block_table[ctx]
    positions = (
        own_blocks[:, :, None, None] * BLOCK
        + piece[:, None, :, None] * half_rows
        + jnp.arange(half_rows, dtype=jnp.int32)
    ).reshape(-1)
    flat = block_table.reshape(-1)
    count = flat.shape[0]
    ids = jnp.arange(count, dtype=jnp.int32)
    place = jnp.sum(jnp.where(flat[None, :] == ids[:, None], ids[None, :], 0), axis=1)
    pair = jnp.bitwise_xor((place // 2) % 2, low)
    order = (place // 4) * 8 + pair * 2 + place % 2
    flips = jnp.where(pair == 0, members[0] // 2, members[2] // 2)
    first = jnp.where(own_blocks[0, 0] < own_blocks[1, 0], 0, 1)
    ends = jnp.sort(own_blocks.reshape(-1))
    source = jnp.stack([2 * first, 2 - 2 * first, 3 - 2 * first, 2 * first + 1]).astype(jnp.int32)
    rotary = 10000.0 ** (-np.arange(0, ROT, 2, dtype=np.float64) / ROT)
    frequency = np.zeros((1, LANES), np.float32)
    frequency[0, :ROT] = np.concatenate([rotary, rotary])
    sign = np.zeros((1, LANES), np.float32)
    sign[0, :ROT] = np.repeat([-1.0, 1.0], ROT // 2)
    angles = positions.astype(jnp.float32)[:, None] * frequency
    cosine = jnp.cos(angles)
    sine = jnp.sin(angles) * sign

    normed, _ = norm_parts(tokens.astype(jnp.float32))
    first_in = (normed * attn_gain_all + attn_shift_all).astype(jnp.bfloat16)
    second_in = (normed * mlp_gain_all + mlp_shift_all).astype(jnp.bfloat16)
    qkv_bias_slice = qkv_bias_slice.astype(jnp.bfloat16)

    def projection(weight, bias, spread):
        weight = dot(weight, spread).astype(jnp.bfloat16)
        projected = dot(first_in, weight) + dot(bias, spread)
        lanes = OWN * LANES
        turned = [
            projected[:, at : at + LANES] * cosine + projected[:, lanes + at : lanes + at + LANES] * sine
            for at in range(0, lanes, LANES)
        ]
        return jnp.concatenate(turned, axis=1), weight[:, :lanes]

    key_value, key_weight = projection(key_slice, qkv_bias_slice[:, WIDE:], SPREAD_KEYS)
    key_value = key_value.astype(jnp.bfloat16)
    key_all = gathered_keys(key_value)
    queries, query_weight = projection(query_slice, qkv_bias_slice[:, :WIDE], SPREAD_QUERIES)
    queries = (queries * HEAD**-0.5).astype(jnp.bfloat16)
    spread_weight = jnp.concatenate([query_weight, key_weight], axis=1)

    pre_act = dot(second_in, up_slice) + up_bias_slice
    cdf_part = 0.5 * (1.0 + lax.erf(pre_act * (1.0 / math.sqrt(2.0))))
    density = jnp.exp(-0.5 * pre_act * pre_act) * (1.0 / math.sqrt(2.0 * math.pi))
    activated = (pre_act * cdf_part).astype(jnp.bfloat16)
    grad_act = times_transposed(cot, down_slice)
    grad_pre_wide = grad_act * (cdf_part + pre_act * density)
    grad_pre = grad_pre_wide.astype(jnp.bfloat16)
    grad_up = outer_sum(second_in, grad_pre).astype(jnp.bfloat16).reshape(32, -1, D)
    grad_down = outer_sum(activated, cot).astype(jnp.bfloat16).reshape(32, -1, D)
    grad_up_bias = jnp.sum(grad_pre.astype(jnp.float32), axis=0)
    second_part = times_transposed(grad_pre, up_slice)
    mlp_part = dot(activated, down_slice)
    second_sums = [jnp.sum(second_part * normed, axis=0), jnp.sum(second_part, axis=0)]
    bias_grad = jnp.sum(cot.astype(jnp.float32), axis=0)

    dense_spread = lax.dot_general(
        dense_slice, LATE_HALF, (((0,), (0,)), ((), ())), preferred_element_type=jnp.float32
    ).astype(jnp.bfloat16)
    grad_heads = dot(cot, dense_spread).astype(jnp.bfloat16)
    queries, grad_heads, grad_up, grad_down, second_part, mlp_part = lax.optimization_barrier(
        (queries, grad_heads, grad_up, grad_down, second_part, mlp_part)
    )
    queries, grad_up, key_all = lax.optimization_barrier((queries, grad_up, key_all))
    up_sum = plane_sum(grad_up)
    grad_second = scattered_tokens(second_part)
    side = core.reshape(1).astype(jnp.int32)

    def one_head(head, queries):
        return attend(
            head, order, flips, ends, source, side, positions.reshape(1, -1), queries, grad_heads, key_all
        )

    out0, query0, kept0, sent0 = one_head(0, queries)
    queries, out0, up_sum, grad_down = lax.optimization_barrier((queries, out0, up_sum, grad_down))
    down_sum = plane_sum(grad_down)
    kept0, down_sum = lax.optimization_barrier((kept0, down_sum))
    out1, query1, kept1, sent1 = one_head(1, queries)
    chip0 = chip_sum(kept0, other_core(sent0))
    queries, out1, chip0 = lax.optimization_barrier((queries, out1, chip0))
    out2, query2, kept2, sent2 = one_head(2, queries)
    key0 = scattered_keys(chip0)
    chip1 = chip_sum(kept1, other_core(sent1))
    sent2, chip1, key0 = lax.optimization_barrier((sent2, chip1, key0))
    chip2 = chip_sum(kept2, other_core(sent2))
    key1 = scattered_keys(chip1)
    chip2, key1 = lax.optimization_barrier((chip2, key1))
    key2 = scattered_keys(chip2)
    attended = [o.astype(jnp.bfloat16) for o in (out0, out1, out2)]
    query_grads, key_grads = [query0, query1, query2], [key0, key1, key2]
    attended = jnp.concatenate(attended, axis=0)
    wide_input = hidden.astype(jnp.float32)
    attn_part = outer_sum(attended, dense_slice)
    layer_out = wide_input + scattered_tokens(attn_part + mlp_part) + (dense_bias_all + down_bias_all)
    padded_attended = dot(PADDED[:WIDE, : WIDE // 6 * 8].T, attended).astype(jnp.bfloat16)
    grad_dense = dot(padded_attended, cot).reshape(32, -1, D)
    line = jnp.pad(grad_up_bias.reshape(32, 1, -1), ((0, 0), (6, 1), (0, D - D // 32)))
    block_sums = to_block_owners(plane_sum((grad_dense + line).astype(jnp.bfloat16)))
    grad_dense_own = block_sums[:6]
    up_bias_own = block_sums[6, : D // 32]

    def turned_back(grad):
        return (
            grad.astype(jnp.float32) * cosine - dot(grad, PARTNER) * sine
        ).astype(jnp.bfloat16)

    padded_in = padded_rows(first_in)
    early = jnp.concatenate([turned_back(g) for g in query_grads + key_grads[:-1]], axis=1)
    early_lanes = early.shape[1]
    early_part = times_transposed(early, spread_weight[:, :early_lanes])
    early_grad = outer_sum(padded_in, early).astype(jnp.bfloat16).reshape(-1, 8, early_lanes)
    early_part, early_grad, last = lax.optimization_barrier((early_part, early_grad, key_grads[-1]))
    late = turned_back(last)
    first_part = early_part + times_transposed(late, spread_weight[:, early_lanes:D])
    grad_first = scattered_tokens(first_part)

    def natural(lanes):
        by_head = lanes.reshape(*lanes.shape[:-1], 2 * OWN, 2, HEAD)
        parts = [by_head[..., :OWN, 0, :], by_head[..., OWN:, 0, :], by_head[..., OWN:, 1, :]]
        return jnp.stack([p.reshape(*lanes.shape[:-1], WIDE) for p in parts], axis=-2)

    mixed_sum = jnp.concatenate([jnp.sum(g.astype(jnp.float32), axis=0) for g in (early, late)])
    bias_line = lax.dynamic_update_slice_in_dim(
        jnp.zeros((LANES, 18), jnp.float32), natural(mixed_sum).T.reshape(32, 18), 32 * depth, 0
    )
    by_row = [bias_grad, jnp.sum(first_part * normed, axis=0), jnp.sum(first_part, axis=0)] + second_sums
    row_line = jnp.concatenate([v.reshape(-1, 6) for v in by_row], axis=1)
    lines = jnp.stack([jnp.pad(l, ((0, 0), (0, D - l.shape[1]))) for l in (bias_line, row_line)], axis=1)
    late_grad = outer_sum(padded_in, late).astype(jnp.bfloat16).reshape(-1, 8, LANES)
    grad_qkv = jnp.concatenate([early_grad, late_grad], axis=2)
    sums = row_owner_sums(grad_qkv + jnp.pad(lines.astype(jnp.bfloat16), ((0, 0), (6, 0), (0, 0))))
    grad_qkv_own = natural(sums[:, :, :6]).transpose(2, 3, 1, 0, 4).reshape(6, 3 * D)
    qkv_bias_own = jnp.sum(sums[:, :, 6, :18], axis=(0, 1)).reshape(6, 3)
    bias_own = sums[0, 0, 7, :6]
    row_values = jnp.sum(sums[:, :, 7, 6:30], axis=(0, 1)).reshape(4, 6)
    attn_gain_own, attn_shift_own, mlp_gain_own, mlp_shift_own = (row_values[i] for i in range(4))
    grad_up_own = jnp.concatenate(to_row_owners(up_sum, depth, high, core), axis=1)
    grad_down_own = to_block_owners(down_sum)

    own_normed, own_inverse = norm_parts(wide_input)
    input_grad = (
        cotangent.astype(jnp.float32)
        + norm_backward(grad_first, own_normed, own_inverse, attn_gain_all)
        + norm_backward(grad_second, own_normed, own_inverse, mlp_gain_all)
    )
    return (
        layer_out.astype(jnp.bfloat16),
        input_grad.astype(jnp.bfloat16),
        grad_qkv_own,
        qkv_bias_own,
        grad_dense_own,
        bias_own,
        grad_up_own,
        up_bias_own,
        grad_down_own,
        bias_own,
        attn_gain_own,
        attn_shift_own,
        mlp_gain_own,
        mlp_shift_own,
    )


def solution(mesh):
    fine = Mesh(mesh.devices.reshape(SIZES), AXES)
    weight = ("zh", "c")
    matrix, vector, share = P(AXES, None), P(AXES), P(weight, None)
    part = P(weight)
    return jax.shard_map(
        local,
        mesh=fine,
        in_specs=(
            matrix, share, part, share, part, share, part, share, part, part, part, part, part, P(), matrix,
        ),
        out_specs=(
            matrix, matrix, matrix, matrix, matrix, vector, matrix, vector, matrix,
            vector, vector, vector, vector, vector,
        ),
        check_vma=False,
    )
```
